256 devices in a mesh: grp: 4 (over y_lo, core), resp: 8 (over x, y_hi), head: 8 (over z).
Axes of the slice: x: 4, y: 4 (y_hi: 2, y_lo: 2; y = y_hi * 2 + y_lo), z: 8, core: 2. Of those that a mesh axis runs over, the one named last changes fastest.
Arguments:
- resp_hidden: bfloat16 [32, 128, 5120], P(('grp', 'resp')), parts along dimension 0, may hold values from -6 to 6
- prompt_hidden: bfloat16 [4096, 5120], P(('grp', 'resp')), parts along dimension 0, may hold values from -6 to 6
- readout: bfloat16 [32, 128, 5120], P(('grp', 'resp')), parts along dimension 0, may hold values from -0.078125 to 0.078125
- query_weight: bfloat16 [5120, 8192], P('resp', 'head'), may hold values from -0.078125 to 0.078125
- key_weight: bfloat16 [5120, 1024], P('resp', 'head'), may hold values from -0.078125 to 0.078125
- value_weight: bfloat16 [5120, 1024], P('resp', 'head'), may hold values from -0.078125 to 0.078125
- out_weight: bfloat16 [5120, 8192], P('resp', 'head'), may hold values from -0.0625 to 0.0625
- query_gain: float32 [128], replicated, may hold values from 0.25 to 1.75
- key_gain: float32 [128], replicated, may hold values from 0.25 to 1.75
- base_logprob: float32 [32, 128], P(('grp', 'resp')), parts along dimension 0, may hold values from -3 to -0.5
- behavior_logprob: float32 [32, 128], P(('grp', 'resp')), parts along dimension 0, may hold values from -4 to 0.5
- reference_logprob: float32 [32, 128], P(('grp', 'resp')), parts along dimension 0, may hold values from -3 to -0.5
- rewards: float32 [32], P(('grp', 'resp')), parts along dimension 0, may hold values from 0.3 to 15.3, as said below
- lengths: int32 [32], P(('grp', 'resp')), parts along dimension 0, may hold values from 1 to 128, as said below
Outputs:
- policy_logprob: float32 [32, 128], P(('grp', 'resp')), parts along dimension 0
- group_loss: float32 [4], P('grp'), parts along dimension 0
- query_grad: bfloat16 [20480, 8192], P(('grp', 'resp'), 'head'), parts along dimension 0
- key_grad: bfloat16 [20480, 1024], P(('grp', 'resp'), 'head'), parts along dimension 0
- value_grad: bfloat16 [20480, 1024], P(('grp', 'resp'), 'head'), parts along dimension 0
- out_grad: bfloat16 [20480, 8192], P(('grp', 'resp'), 'head'), parts along dimension 0
The draws below stay inside these ranges and needn't reach their ends.
There are 4 independent parts, one for each index of `grp`. The reference program is written for one: setup_inputs(seed, part) draws one part's arguments, and reference() takes and returns one part's arrays. A program takes and returns all parts, laid end to end along the dimension named above; an argument that names none is the same for every part. Nothing has to cross between parts.
Inputs may be any that keep to these rules, and one draw needn't show every extreme that they name: `lengths`: a response's live tokens come first; later positions are padding. `rewards`: scalar reward of a response.
All inputs are finite; a program needn't handle non-finite values.
Results may differ from the reference program's by a relative error of at most 0.023.
Values may be sent and summed in bfloat16 or wider, within the bound.
No kernel may reach another device: no remote copies, remote signals or barrier semaphores. Data moves between devices by JAX's collectives and lax.ppermute only.
A program may use at most 128 MiB of HBM per device.

```python
import math
import jax
import jax.numpy as jnp
from jax import lax

D = 5120
HD = 128
HQ = 64
KVH = 8
RT = 128
PT_DEV = 128
RESPS = 8
PTOK = 1024


def draw_rewards(key, part):
    key = jax.random.fold_in(key, 11)
    position = jnp.arange(RESPS, dtype=jnp.float32) / max(RESPS - 1, 1)
    return (1.0 + 2.0 * position) * jax.random.uniform(key, (RESPS,), jnp.float32, 0.5, 1.5)


def draw_lengths(key, part):
    key = jax.random.fold_in(key, 23)
    first_key, second_key = jax.random.split(key)
    drawn = jax.random.randint(first_key, (RESPS,), 1, RT + 1)
    longest = jax.random.randint(second_key, (), 0, RESPS)
    return jnp.where(jnp.arange(RESPS) == longest, RT, drawn).astype(jnp.int32)


def level_of(own_key, extent, pieces, least, largest):
    loudness = 1.0
    for axis_at, shards_of in pieces:
        draws = jax.random.uniform(jax.random.fold_in(jax.random.fold_in(own_key, 6), axis_at), (shards_of,), jnp.float32, least / len(pieces), largest / len(pieces))
        loudness = loudness * jnp.repeat(jnp.exp(draws), extent[axis_at] // shards_of).reshape((-1,) + (1,) * (len(extent) - 1 - axis_at))
    return loudness


def bell_draw(own_key, dims, scale, reach, cuts=(), held_as=jnp.bfloat16):
    array = scale * jax.random.normal(own_key, dims, jnp.float32)
    if cuts:
        array = array * level_of(own_key, dims, cuts, -0.22, 0.18)
    return jnp.clip(array, -reach, reach).astype(held_as)


def setup_inputs(seed: int = 0, part: int = 0) -> dict:
    streams_of = jax.random.split(jax.random.key(seed), 15)
    part_keys = jax.random.split(jax.random.fold_in(streams_of[14], part), 15)
    return {
        "resp_hidden": bell_draw(part_keys[0], (RESPS, RT, D), 1.0, 6.0, ((0, 8),)),
        "prompt_hidden": bell_draw(part_keys[1], (PTOK, D), 1.0, 6.0, ((0, 8),)),
        "readout": bell_draw(part_keys[2], (RESPS, RT, D), D ** -0.5, 0.078125, ((0, 8),)),
        "query_weight": bell_draw(streams_of[3], (D, HQ * HD), D ** -0.5, 0.078125, ((0, 8), (1, 8))),
        "key_weight": bell_draw(streams_of[4], (D, KVH * HD), D ** -0.5, 0.078125, ((0, 8), (1, 8))),
        "value_weight": bell_draw(streams_of[5], (D, KVH * HD), D ** -0.5, 0.078125, ((0, 8), (1, 8))),
        "out_weight": bell_draw(streams_of[6], (D, HQ * HD), (HQ * HD) ** -0.5, 0.0625, ((0, 8), (1, 8))),
        "query_gain": jnp.clip(1.0 + 0.15 * jax.random.normal(streams_of[7], (HD,), jnp.float32), 0.25, 1.75),
        "key_gain": jnp.clip(1.0 + 0.15 * jax.random.normal(streams_of[8], (HD,), jnp.float32), 0.25, 1.75),
        "base_logprob": jnp.clip(-3.0 + 2.5 * jax.random.uniform(part_keys[9], (RESPS, RT), jnp.float32) ** level_of(part_keys[9], (RESPS, RT), ((0, 8),), -0.2, 0.2), -3.0, -0.5),
        "behavior_logprob": jnp.clip(-4.0 + 4.5 * jax.random.uniform(part_keys[10], (RESPS, RT), jnp.float32) ** level_of(part_keys[10], (RESPS, RT), ((0, 8),), -0.2, 0.2), -4.0, 0.5),
        "reference_logprob": jnp.clip(-3.0 + 2.5 * jax.random.uniform(part_keys[11], (RESPS, RT), jnp.float32) ** level_of(part_keys[11], (RESPS, RT), ((0, 8),), -0.2, 0.2), -3.0, -0.5),
        "rewards": draw_rewards(jax.random.fold_in(jax.random.fold_in(streams_of[14], part), 71), part),
        "lengths": draw_lengths(jax.random.fold_in(jax.random.fold_in(streams_of[14], part), 71), part),
    }


norm_eps = 1e-06
rope_base = 1000000.0
clip_low = 0.8
clip_high = 1.28
kl_weight = 0.04

def norm_rope(values, scale_gain, positions):
    row_count = values.shape[0]
    head_count = values.shape[1] // HD
    shaped = values.reshape(row_count, head_count, HD)
    mean_square = lax.optimization_barrier(jnp.mean(shaped * shaped, axis=-1, keepdims=True))
    normed = shaped * lax.rsqrt(mean_square + norm_eps) * scale_gain
    half_dim = HD // 2
    frequency = jnp.exp(jnp.arange(half_dim, dtype=jnp.float32) * (-2.0 * math.log(rope_base) / HD))
    angles = positions[:, None] * frequency[None, :]
    cosine_table = jnp.cos(angles)[:, None, :]
    sine_table = jnp.sin(angles)[:, None, :]
    first_half = normed[..., :half_dim]
    second_half = normed[..., half_dim:]
    rotated = jnp.concatenate([first_half * cosine_table - second_half * sine_table, second_half * cosine_table + first_half * sine_table], axis=-1)
    return rotated.reshape(row_count, head_count * HD)

def rope_back(pre_values, scale_gain, positions, cotangent):
    result = jax.vjp(lambda inner_values: norm_rope(inner_values, scale_gain, positions), pre_values)[1](cotangent)
    return result[0]

def seen_mask(query_count, key_count, prompt_count):
    query_index = jnp.arange(query_count)[:, None]
    key_index = jnp.arange(key_count)[None, :]
    return (key_index < prompt_count) | (key_index - prompt_count <= query_index)

def split_heads(query, keys, values):
    row_count = query.shape[0]
    key_count = keys.shape[0]
    kv_heads = keys.shape[1] // HD
    group_size = query.shape[1] // keys.shape[1]
    query_heads = query.astype(jnp.float32).reshape(row_count, kv_heads, group_size, HD)
    key_heads = keys.astype(jnp.float32).reshape(key_count, kv_heads, HD)
    value_heads = values.astype(jnp.float32).reshape(key_count, kv_heads, HD)
    return (query_heads, key_heads, value_heads)

def attend(query, keys, values, prompt_count):
    query_heads, key_heads, value_heads = split_heads(query, keys, values)
    row_count = query.shape[0]
    scores = jnp.einsum('tkgh,nkh->kgtn', query_heads, key_heads) * HD ** (-0.5)
    weights = jnp.where(seen_mask(row_count, keys.shape[0], prompt_count), jnp.exp(scores), 0.0)
    probs = weights / lax.optimization_barrier(jnp.sum(weights, axis=-1, keepdims=True))
    probs_low = probs.astype(jnp.bfloat16)
    mixed = jnp.einsum('kgtn,nkh->tkgh', probs_low.astype(jnp.float32), value_heads)
    return (mixed.reshape(row_count, -1).astype(jnp.bfloat16), probs, probs_low)

def attend_back(query, keys, values, probs, probs_low, grad_low):
    query_heads, key_heads, value_heads = split_heads(query, keys, values)
    row_count = query.shape[0]
    key_count = keys.shape[0]
    grad_heads = grad_low.astype(jnp.float32).reshape(query_heads.shape)
    value_cot = jnp.einsum('kgtn,tkgh->nkh', probs_low.astype(jnp.float32), grad_heads)
    prob_cot = jnp.einsum('tkgh,nkh->kgtn', grad_heads, value_heads)
    inner_sum = lax.optimization_barrier(jnp.sum(probs * prob_cot, axis=-1, keepdims=True))
    score_cot = (probs * (prob_cot - inner_sum) * HD ** (-0.5)).astype(jnp.bfloat16)
    query_cot = jnp.einsum('kgtn,nkh->tkgh', score_cot.astype(jnp.float32), key_heads).reshape(row_count, -1)
    key_cot = jnp.einsum('kgtn,tkgh->nkh', score_cot.astype(jnp.float32), query_heads).reshape(key_count, -1)
    return (query_cot, key_cot, value_cot.reshape(key_count, -1))

def objective(logprob, behavior, reference_lp, advantage, live):
    ratios = jnp.exp(logprob - behavior)
    weight = jnp.clip(ratios, clip_low, clip_high)
    ref_gap = reference_lp - logprob
    penalty = jnp.exp(ref_gap) - ref_gap - 1.0
    token_loss = live * (kl_weight * penalty - weight * advantage * logprob)
    lp_slope = live * (kl_weight * (1.0 - jnp.exp(ref_gap)) - weight * advantage)
    return (jnp.sum(token_loss), lp_slope)

def reference(resp_hidden, prompt_hidden, readout, query_weight, key_weight, value_weight, out_weight, query_gain, key_gain, base_logprob, behavior_logprob, reference_logprob, rewards, lengths):
    kp_pre = jnp.dot(prompt_hidden, key_weight, preferred_element_type=jnp.float32)
    vp_pre = jnp.dot(prompt_hidden, value_weight, preferred_element_type=jnp.float32)
    prompt_pos = jnp.arange(PTOK).astype(jnp.float32)
    resp_pos = (PTOK + jnp.arange(RT)).astype(jnp.float32)
    prompt_keys = norm_rope(kp_pre, key_gain, prompt_pos).astype(jnp.bfloat16)
    prompt_values = vp_pre.astype(jnp.bfloat16)
    mean_reward = jnp.sum(rewards) / RESPS

    def one_response(which):
        own_x = resp_hidden[which]
        own_read = readout[which]
        q_pre = jnp.dot(own_x, query_weight, preferred_element_type=jnp.float32)
        kr_pre = jnp.dot(own_x, key_weight, preferred_element_type=jnp.float32)
        vr_pre = jnp.dot(own_x, value_weight, preferred_element_type=jnp.float32)
        mixing = jnp.dot(own_read, out_weight, preferred_element_type=jnp.float32)
        query = norm_rope(q_pre, query_gain, resp_pos).astype(jnp.bfloat16)
        resp_keys = norm_rope(kr_pre, key_gain, resp_pos).astype(jnp.bfloat16)
        keys = jnp.concatenate([prompt_keys, resp_keys], axis=0)
        values = jnp.concatenate([prompt_values, vr_pre.astype(jnp.bfloat16)], axis=0)
        mixed, probs, probs_low = attend(query, keys, values, PTOK)
        attn_part = lax.optimization_barrier(jnp.sum(mixed.astype(jnp.float32) * mixing, axis=-1))
        own_part = lax.optimization_barrier(jnp.sum(own_x.astype(jnp.float32) * own_read.astype(jnp.float32), axis=-1))
        logprob = base_logprob[which] + own_part + attn_part
        live = (jnp.arange(RT) < lengths[which]).astype(jnp.float32)
        loss_own, lp_slope = objective(logprob, behavior_logprob[which], reference_logprob[which], rewards[which] - mean_reward, live)
        mixed_grad = (lp_slope[:, None] * mixing).astype(jnp.bfloat16)
        mixing_grad = (lp_slope[:, None] * mixed.astype(jnp.float32)).astype(jnp.bfloat16)
        query_cot, key_cot, value_cot = attend_back(query, keys, values, probs, probs_low, mixed_grad)
        dq_low = rope_back(q_pre, query_gain, resp_pos, query_cot).astype(jnp.bfloat16)
        dkr_low = rope_back(kr_pre, key_gain, resp_pos, key_cot[PTOK:]).astype(jnp.bfloat16)
        dvr_low = value_cot[PTOK:].astype(jnp.bfloat16)
        return (logprob, loss_own, dq_low, dkr_low, dvr_low, mixing_grad, key_cot[:PTOK], value_cot[:PTOK])
    results = lax.map(one_response, jnp.arange(RESPS).astype(jnp.int32))
    logprobs, losses, dq_all, dkr_all, dvr_all, mixing_all, key_parts, value_parts = results
    dkp_low = rope_back(kp_pre, key_gain, prompt_pos, lax.optimization_barrier(jnp.sum(key_parts, axis=0))).astype(jnp.bfloat16)
    dvp_low = lax.optimization_barrier(jnp.sum(value_parts, axis=0)).astype(jnp.bfloat16)

    def accumulate(totals, which):
        own_x = resp_hidden[which]
        own_read = readout[which]
        first_row = (which * PT_DEV).astype(jnp.int32)
        prompt_rows = lax.dynamic_slice_in_dim(prompt_hidden, first_row, PT_DEV, 0)
        dkp_rows = lax.dynamic_slice_in_dim(dkp_low, first_row, PT_DEV, 0)
        dvp_rows = lax.dynamic_slice_in_dim(dvp_low, first_row, PT_DEV, 0)
        term = jnp.concatenate([jnp.dot(own_x.T, dq_all[which], preferred_element_type=jnp.float32), jnp.dot(own_x.T, dkr_all[which], preferred_element_type=jnp.float32) + jnp.dot(prompt_rows.T, dkp_rows, preferred_element_type=jnp.float32), jnp.dot(own_x.T, dvr_all[which], preferred_element_type=jnp.float32) + jnp.dot(prompt_rows.T, dvp_rows, preferred_element_type=jnp.float32), jnp.dot(own_read.T, mixing_all[which], preferred_element_type=jnp.float32)], axis=1)
        term = lax.optimization_barrier(term.astype(jnp.bfloat16)).astype(jnp.float32)
        return (totals + term, None)
    start_total = jnp.zeros((D, 2 * HQ * HD + 2 * KVH * HD), jnp.float32)
    summed, _ = lax.scan(accumulate, start_total, jnp.arange(RESPS).astype(jnp.int32))
    q_end = HQ * HD
    k_end = q_end + KVH * HD
    v_end = k_end + KVH * HD
    return (logprobs, jnp.sum(losses).reshape(1), summed[:, :q_end].astype(jnp.bfloat16), summed[:, q_end:k_end].astype(jnp.bfloat16), summed[:, k_end:v_end].astype(jnp.bfloat16), summed[:, v_end:].astype(jnp.bfloat16))
```

```python
import math

import jax
import jax.numpy as jnp
from jax import lax
from jax.sharding import PartitionSpec as P

HD = 128


norm_eps = 1e-06
rope_base = 1000000.0
clip_low = 0.8
clip_high = 1.28
kl_weight = 0.04


def norm_rope(values, scale_gain, positions):
    row_count = values.shape[0]
    head_count = values.shape[1] // HD
    shaped = values.reshape(row_count, head_count, HD)
    mean_square = jnp.mean(shaped * shaped, axis=-1, keepdims=True)
    normed = shaped * lax.rsqrt(mean_square + norm_eps) * scale_gain
    half_dim = HD // 2
    frequency = jnp.exp(jnp.arange(half_dim, dtype=jnp.float32) * (-2.0 * math.log(rope_base) / HD))
    angles = positions[:, None] * frequency[None, :]
    cosine_table = jnp.cos(angles)[:, None, :]
    sine_table = jnp.sin(angles)[:, None, :]
    first_half = normed[..., :half_dim]
    second_half = normed[..., half_dim:]
    rotated = jnp.concatenate(
        [
            first_half * cosine_table - second_half * sine_table,
            second_half * cosine_table + first_half * sine_table,
        ],
        axis=-1,
    )
    return rotated.reshape(row_count, head_count * HD)


def rope_back(pre_values, scale_gain, positions, cotangent):
    result = jax.vjp(
        lambda inner_values: norm_rope(inner_values, scale_gain, positions), pre_values
    )[1](cotangent)
    return result[0]


def seen_mask(query_count, key_count, prompt_count):
    query_index = jnp.arange(query_count)[:, None]
    key_index = jnp.arange(key_count)[None, :]
    return (key_index < prompt_count) | (key_index - prompt_count <= query_index)


def split_heads(query, keys, values):
    row_count = query.shape[0]
    key_count = keys.shape[0]
    kv_heads = keys.shape[1] // HD
    group_size = query.shape[1] // keys.shape[1]
    query_heads = query.reshape(row_count, kv_heads, group_size, HD)
    key_heads = keys.reshape(key_count, kv_heads, HD)
    value_heads = values.reshape(key_count, kv_heads, HD)
    return (query_heads, key_heads, value_heads)


def attend(query, keys, values, prompt_count):
    query_heads, key_heads, value_heads = split_heads(query, keys, values)
    row_count = query.shape[0]
    scores = jnp.einsum(
        "tkgh,nkh->kgtn", query_heads, key_heads, preferred_element_type=jnp.float32
    ) * HD ** (-0.5)
    weights = jnp.where(seen_mask(row_count, keys.shape[0], prompt_count), jnp.exp(scores), 0.0)
    probs = weights / jnp.sum(weights, axis=-1, keepdims=True)
    probs_low = probs.astype(jnp.bfloat16)
    mixed = jnp.einsum("kgtn,nkh->tkgh", probs_low, value_heads, preferred_element_type=jnp.float32)
    return (mixed.reshape(row_count, -1).astype(jnp.bfloat16), probs, probs_low)


def attend_back(query, keys, values, probs, probs_low, grad_low):
    query_heads, key_heads, value_heads = split_heads(query, keys, values)
    row_count = query.shape[0]
    key_count = keys.shape[0]
    grad_heads = grad_low.reshape(query_heads.shape)
    value_cot = jnp.einsum(
        "kgtn,tkgh->nkh", probs_low, grad_heads, preferred_element_type=jnp.float32
    )
    prob_cot = jnp.einsum(
        "tkgh,nkh->kgtn", grad_heads, value_heads, preferred_element_type=jnp.float32
    )
    inner_sum = jnp.sum(probs * prob_cot, axis=-1, keepdims=True)
    score_cot = (probs * (prob_cot - inner_sum) * HD ** (-0.5)).astype(jnp.bfloat16)
    query_cot = jnp.einsum(
        "kgtn,nkh->tkgh", score_cot, key_heads, preferred_element_type=jnp.float32
    ).reshape(row_count, -1)
    key_cot = jnp.einsum(
        "kgtn,tkgh->nkh", score_cot, query_heads, preferred_element_type=jnp.float32
    ).reshape(key_count, -1)
    return (query_cot, key_cot, value_cot.reshape(key_count, -1))


def objective(logprob, behavior, reference_lp, advantage, live):
    ratios = jnp.exp(logprob - behavior)
    weight = jnp.clip(ratios, clip_low, clip_high)
    ref_gap = reference_lp - logprob
    penalty = jnp.exp(ref_gap) - ref_gap - 1.0
    token_loss = live * (kl_weight * penalty - weight * advantage * logprob)
    lp_slope = live * (kl_weight * (1.0 - jnp.exp(ref_gap)) - weight * advantage)
    return (jnp.sum(token_loss), lp_slope)


def swap_sum(value, axis):
    size = lax.axis_size(axis)
    step = 1
    while step < size:
        value = value + lax.ppermute(value, axis, [(i, i ^ step) for i in range(size)])
        step *= 2
    return value


def exchange(blocks):
    return lax.all_to_all(blocks, "resp", split_axis=0, concat_axis=0, tiled=True)


def spread(block, groups):
    return exchange(jnp.broadcast_to(block[None], (groups,) + block.shape))


def body(
    resp_hidden,
    prompt_hidden,
    readout,
    query_weight,
    key_weight,
    value_weight,
    out_weight,
    query_gain,
    key_gain,
    base_logprob,
    behavior_logprob,
    reference_logprob,
    rewards,
    lengths,
):
    own_x = resp_hidden[0]
    own_read = readout[0]
    rows = own_x.shape[0]
    qcols = query_weight.shape[1]
    kcols = key_weight.shape[1]
    groups = lax.axis_size("resp")
    index = lax.axis_index("resp")
    width = own_x.shape[1] // groups
    bf16 = jnp.bfloat16

    reward_sum = swap_sum(rewards, "resp")[0]
    tokens = jnp.concatenate([own_x, prompt_hidden, own_read], axis=0)
    tokens = exchange(tokens.reshape(3 * rows, groups, width).transpose(1, 0, 2))
    cols_x = tokens[:, :rows]
    cols_p = tokens[:, rows : 2 * rows]
    cols_r = tokens[:, 2 * rows :]

    def project(left, right):
        return jnp.einsum("ntd,dc->ntc", left, right, preferred_element_type=jnp.float32).astype(bf16)

    partial_terms = jnp.concatenate(
        [
            project(cols_x, query_weight),
            project(cols_r, out_weight),
            project(cols_x, key_weight),
            project(cols_x, value_weight),
            project(cols_p, key_weight),
            project(cols_p, value_weight),
        ],
        axis=2,
    )
    sums = jnp.sum(exchange(partial_terms).astype(jnp.float32), axis=0)
    q_pre = sums[:, :qcols]
    mixing = sums[:, qcols : 2 * qcols]
    kr_pre, vr_pre, kp_pre, vp_pre = (
        sums[:, 2 * qcols + n * kcols : 2 * qcols + (n + 1) * kcols] for n in range(4)
    )
    prompt_pos = (index * rows + jnp.arange(rows)).astype(jnp.float32)
    resp_pos = (rows * groups + jnp.arange(rows)).astype(jnp.float32)
    prompt_keys = norm_rope(kp_pre, key_gain, prompt_pos).astype(bf16)
    prompt_kv = spread(jnp.concatenate([prompt_keys, vp_pre.astype(bf16)], axis=1), groups)
    prompt_count = rows * groups
    prompt_kv = prompt_kv.reshape(prompt_count, 2 * kcols)
    query = norm_rope(q_pre, query_gain, resp_pos).astype(bf16)
    resp_keys = norm_rope(kr_pre, key_gain, resp_pos).astype(bf16)
    keys = jnp.concatenate([prompt_kv[:, :kcols], resp_keys], axis=0)
    values = jnp.concatenate([prompt_kv[:, kcols:], vr_pre.astype(bf16)], axis=0)
    mixed, probs, probs_low = attend(query, keys, values, prompt_count)
    mixed_wide = mixed.astype(jnp.float32)
    attn_part = jnp.sum(mixed_wide * mixing, axis=-1)
    own_part = jnp.einsum("td,td->t", own_x, own_read, preferred_element_type=jnp.float32)
    attn_logit = swap_sum(attn_part[None, :], "head")[0]
    logprob = base_logprob[0] + own_part + attn_logit
    advantage = rewards[0] - reward_sum / groups
    live = (jnp.arange(rows) < lengths[0]).astype(jnp.float32)
    loss_own, lp_slope = objective(
        logprob, behavior_logprob[0], reference_logprob[0], advantage, live
    )
    group_loss = swap_sum(loss_own.reshape(1), "resp")
    mixed_grad = (lp_slope[:, None] * mixing).astype(bf16)
    mixing_grad = (lp_slope[:, None] * mixed_wide).astype(bf16)
    query_cot, key_cot, value_cot = attend_back(query, keys, values, probs, probs_low, mixed_grad)
    prompt_cots = jnp.concatenate(
        [key_cot[:prompt_count].astype(bf16), value_cot[:prompt_count].astype(bf16)], axis=1
    )
    prompt_cots = jnp.sum(
        exchange(prompt_cots.reshape(groups, rows, 2 * kcols)).astype(jnp.float32), axis=0
    )
    dkp_low = rope_back(kp_pre, key_gain, prompt_pos, prompt_cots[:, :kcols]).astype(bf16)
    dvp_low = prompt_cots[:, kcols:].astype(bf16)
    dq_low = rope_back(q_pre, query_gain, resp_pos, query_cot).astype(bf16)
    dkr_low = rope_back(kr_pre, key_gain, resp_pos, key_cot[prompt_count:]).astype(bf16)
    dvr_low = value_cot[prompt_count:].astype(bf16)
    cots = spread(
        jnp.concatenate([dq_low, mixing_grad, dkr_low, dvr_low, dkp_low, dvp_low], axis=1), groups
    )

    def weight_grad(left, right):
        return jnp.einsum("ntd,ntc->dc", left, right, preferred_element_type=jnp.float32)

    kv_grad = weight_grad(cols_x, cots[:, :, 2 * qcols : 2 * qcols + 2 * kcols]) + weight_grad(
        cols_p, cots[:, :, 2 * qcols + 2 * kcols :]
    )
    return (
        logprob[None, :],
        group_loss,
        weight_grad(cols_x, cots[:, :, :qcols]).astype(bf16),
        kv_grad[:, :kcols].astype(bf16),
        kv_grad[:, kcols:].astype(bf16),
        weight_grad(cols_r, cots[:, :, qcols : 2 * qcols]).astype(bf16),
    )


def solution(mesh):
    placed = (
        P(("grp", "resp"), None, None),
        P(("grp", "resp"), None),
        P(("grp", "resp"), None, None),
        P("resp", "head"),
        P("resp", "head"),
        P("resp", "head"),
        P("resp", "head"),
        P(),
        P(),
        P(("grp", "resp"), None),
        P(("grp", "resp"), None),
        P(("grp", "resp"), None),
        P(("grp", "resp")),
        P(("grp", "resp")),
    )
    return jax.shard_map(
        body,
        mesh=mesh,
        in_specs=placed,
        out_specs=(
            P(("grp", "resp"), None),
            P("grp"),
            P(("grp", "resp"), "head"),
            P(("grp", "resp"), "head"),
            P(("grp", "resp"), "head"),
            P(("grp", "resp"), "head"),
        ),
        check_vma=False,
    )
```

```python
import math

import jax
import jax.numpy as jnp
from jax import lax
from jax.experimental import pallas as pl
from jax.experimental.pallas import tpu as pltpu
from jax.sharding import PartitionSpec as P

HD = 128


norm_eps = 1e-06
rope_base = 1000000.0
clip_low = 0.8
clip_high = 1.28
kl_weight = 0.04


def norm_rope(values, scale_gain, positions):
    row_count = values.shape[0]
    head_count = values.shape[1] // HD
    shaped = values.reshape(row_count, head_count, HD)
    mean_square = jnp.mean(shaped * shaped, axis=-1, keepdims=True)
    normed = shaped * lax.rsqrt(mean_square + norm_eps) * scale_gain
    half_dim = HD // 2
    frequency = jnp.exp(jnp.arange(half_dim, dtype=jnp.float32) * (-2.0 * math.log(rope_base) / HD))
    angles = positions[:, None] * frequency[None, :]
    cosine_table = jnp.cos(angles)[:, None, :]
    sine_table = jnp.sin(angles)[:, None, :]
    first_half = normed[..., :half_dim]
    second_half = normed[..., half_dim:]
    rotated = jnp.concatenate(
        [
            first_half * cosine_table - second_half * sine_table,
            second_half * cosine_table + first_half * sine_table,
        ],
        axis=-1,
    )
    return rotated.reshape(row_count, head_count * HD)


def objective(logprob, behavior, reference_lp, advantage, live):
    ratios = jnp.exp(logprob - behavior)
    weight = jnp.clip(ratios, clip_low, clip_high)
    ref_gap = reference_lp - logprob
    penalty = jnp.exp(ref_gap) - ref_gap - 1.0
    token_loss = live * (kl_weight * penalty - weight * advantage * logprob)
    lp_slope = live * (kl_weight * (1.0 - jnp.exp(ref_gap)) - weight * advantage)
    return (jnp.sum(token_loss), lp_slope)


XS = 4
BF = jnp.bfloat16
F32 = jnp.float32
NT = (((1,), (1,)), ((), ()))
TN = (((0,), (0,)), ((), ()))
PAIR = 4
params = pltpu.CompilerParams(vmem_limit_bytes=30 * 1024 * 1024)
alone = pltpu.CompilerParams(vmem_limit_bytes=60 * 1024 * 1024)


TAIL = 16


def cost(us):
    return pl.CostEstimate(flops=int(us * 1e8), bytes_accessed=1 << 18, transcendentals=0)


def wide(value):
    return value.astype(F32)


def sds(shape, dtype):
    return jax.ShapeDtypeStruct(shape, dtype)


def whole(array):
    shape = array.shape
    return pl.BlockSpec(shape, lambda *_: (0,) * len(shape))


def send(value, dx, dy=0):
    pairs = [(x * 2 + y, ((x + dx) % XS) * 2 + (y ^ dy)) for x in range(XS) for y in range(2)]
    return lax.ppermute(value, "resp", pairs)


def xor_sum(value, axis):
    def flip(term, step):
        return lax.ppermute(term, axis, [(i, i ^ step) for i in range(2 * XS)])

    quad = (value + flip(value, 1)) + (flip(value, 2) + flip(value, 3))
    return quad + flip(quad, 4)


def with_scalar(block, scalar):
    high = lax.reduce_precision(scalar, 8, 7)
    rest = scalar - high
    middle = lax.reduce_precision(rest, 8, 7)
    terms = jnp.stack([high, middle, rest - middle]).astype(BF)
    tail = jnp.zeros((TAIL, block.shape[1]), BF).at[0, :3].set(terms)
    return jnp.concatenate([block, tail], axis=0)


def scalar_of(block):
    return jnp.sum(jnp.sum(wide(block[-TAIL:]), axis=0, keepdims=True), axis=1, keepdims=True)


def exchange(blocks):
    return lax.all_to_all(blocks, "resp", split_axis=0, concat_axis=0, tiled=True)


def pack(own_x, own_p, own_r):
    rows, depth = own_x.shape
    width = depth // (2 * XS)

    def kernel(x_ref, p_ref, r_ref, out_ref, acc_ref):
        x, r = x_ref[...], r_ref[...]
        for n in range(2):
            at = slice(n * width, (n + 1) * width)
            out_ref[n, :rows] = x[:, at]
            out_ref[n, rows : 2 * rows] = p_ref[:, at]
            out_ref[n, 2 * rows :] = r[:, at]
        terms = wide(x) * wide(r)
        total = sum(terms[:, n : n + HD] for n in range(0, 2 * width, HD))

        @pl.when(pl.program_id(0) == 0)
        def _():
            acc_ref[...] = total

        @pl.when(pl.program_id(0) > 0)
        def _():
            acc_ref[...] += total

    return pl.pallas_call(
        kernel,
        grid=(XS,),
        out_shape=[sds((2 * XS, 3 * rows, width), BF), sds((rows, HD), F32)],
        in_specs=[pl.BlockSpec((rows, 2 * width), lambda n: (0, n))] * 3,
        out_specs=[
            pl.BlockSpec((2, 3 * rows, width), lambda n: (n, 0, 0)),
            pl.BlockSpec((rows, HD), lambda n: (0, 0)),
        ],
        compiler_params=alone,
        cost_estimate=cost(4),
    )(own_x, own_p, own_r)


def project(order, tokens, parts, weight, by_x):
    width = tokens.shape[2]
    rows = tokens.shape[1] // 3
    cols, tile = weight.shape[1], 256
    count = XS if by_x else 2
    inner = 2 * XS // count
    kinds = sorted(set(parts))
    total = 2 * XS * len(kinds)

    def kernel(order_ref, *refs):
        blocks, weight_ref, outs, lefts = refs[:total], refs[total], refs[total + 1 : -1], refs[-1]
        for n in range(total):
            lefts[n * rows : (n + 1) * rows] = blocks[n][0]
        for c in range(cols // tile):
            at = slice(c * tile, (c + 1) * tile)
            kind = kinds.index(parts[c])
            left = lefts[kind * 2 * XS * rows : (kind + 1) * 2 * XS * rows]
            got = jnp.dot(left, weight_ref[:, at], preferred_element_type=F32).astype(BF)
            for n in range(2 * XS):
                piece = got[n * rows : (n + 1) * rows]
                if by_x:
                    outs[n % XS][n // XS, :, at] = piece
                else:
                    outs[n // XS][n % XS, :, at] = piece

    def block(part, n):
        return pl.BlockSpec((1, rows, width), lambda c, o: (o[n], part, 0))

    return pl.pallas_call(
        kernel,
        grid_spec=pltpu.PrefetchScalarGridSpec(
            num_scalar_prefetch=1,
            grid=(1,),
            in_specs=[block(part, n) for part in kinds for n in range(2 * XS)] + [whole(weight)],
            out_specs=[pl.BlockSpec((inner, rows, cols), lambda c, o: (0, 0, 0))] * count,
            scratch_shapes=[pltpu.VMEM((total * rows, width), BF)],
        ),
        out_shape=[sds((inner, rows, cols), BF)] * count,
        compiler_params=alone,
        cost_estimate=cost(4),
    )(order, *[tokens] * total, weight)


def flip_tokens(order, tokens):
    width = tokens.shape[2]
    rows = tokens.shape[1] // 3

    def kernel(order_ref, tokens_ref, x_ref, p_ref, r_ref):
        x_ref[...] = tokens_ref[0, :rows].T
        p_ref[...] = tokens_ref[0, rows : 2 * rows].T
        r_ref[...] = tokens_ref[0, 2 * rows :].T

    by_offset = pl.BlockSpec((width, rows), lambda s, o: (0, s))
    return pl.pallas_call(
        kernel,
        grid_spec=pltpu.PrefetchScalarGridSpec(
            num_scalar_prefetch=1,
            grid=(2 * XS,),
            in_specs=[pl.BlockSpec((1, 3 * rows, width), lambda s, o: (o[s], 0, 0))],
            out_specs=[by_offset] * 3,
        ),
        out_shape=[sds((width, 2 * XS * rows), BF)] * 3,
        compiler_params=params,
        cost_estimate=cost(8),
    )(order, tokens)


KV_BLOCKS = 2 * XS + 1


def kv_specs(prompt, own_kv):
    rows = own_kv.shape[0] + TAIL
    specs = [pl.BlockSpec((rows, 2 * HD), lambda h: (0, 0))] * 2
    arrays = list(prompt[:2])
    for array in prompt[2:]:
        for n in range(2):
            specs.append(pl.BlockSpec((1, rows, 2 * HD), lambda h, n=n: (n, 0, 0)))
            arrays.append(array)
    return specs + [whole(own_kv)], arrays + [own_kv]


def load_kv(refs, keys, values):
    rows = refs[-1].shape[0]
    for n, ref in enumerate(refs):
        block = ref[...].reshape(-1, 2 * HD)[:rows]
        keys[n * rows : (n + 1) * rows] = block[:, :HD]
        values[n * rows : (n + 1) * rows] = block[:, HD:]


def probabilities(query, keys, rows):
    scores = lax.dot_general(keys, query, NT, preferred_element_type=F32) * HD ** (-0.5)
    weights = jnp.exp(scores)
    key = lax.broadcasted_iota(jnp.int32, (rows, query.shape[0]), 0)
    position = lax.broadcasted_iota(jnp.int32, (rows, query.shape[0]), 1) % rows
    count = keys.shape[0] - rows
    own = jnp.where(key <= position, weights[count:], 0.0)
    weights = jnp.concatenate([weights[:count], own], axis=0)
    return weights * (1.0 / jnp.sum(weights, axis=0, keepdims=True))


def stack_heads(value):
    return jnp.concatenate([value[:, n * HD : (n + 1) * HD] for n in range(PAIR)], axis=0)


def lay_heads(value):
    rows = value.shape[0] // PAIR
    return jnp.concatenate([value[n * rows : (n + 1) * rows] for n in range(PAIR)], axis=1)


def turn(normed, cosine, sine):
    return normed * cosine + pltpu.roll(normed, HD // 2, 1) * sine


def turn_back(pre, gain, cosine, sine, cotangent):
    scale = lax.rsqrt(jnp.mean(pre * pre, axis=-1, keepdims=True) + norm_eps)
    half = HD // 2
    flipped = jnp.concatenate([cotangent[:, half:], cotangent[:, :half]], axis=1)
    inner = (cotangent * cosine - flipped * sine) * gain
    return scale * inner - pre * (scale * scale * scale * jnp.mean(pre * inner, axis=-1, keepdims=True))


def attention(q_first, q_rest, m_pairs, m_last, prompt, own_kv, cosine, sine, gain):
    rows, cols = m_last.shape[0], m_last.shape[1] - 2 * HD
    wide_cols = PAIR * HD
    count = KV_BLOCKS * rows
    specs, arrays = kv_specs(prompt, own_kv)
    stacked = pl.BlockSpec((1, rows, wide_cols), lambda h: (0, 0, h))
    flat = pl.BlockSpec((rows, wide_cols), lambda h: (0, h))

    def kernel(*refs):
        q_in, m_in, rest = refs[:5], refs[5:10], refs[10:]
        kv_in, rest = rest[:KV_BLOCKS], rest[KV_BLOCKS:]
        cos_ref, sin_ref, gain_ref = rest[:3]
        pre_ref, query_ref, mixed_ref, mixing_ref, acc_ref, sum_ref = rest[3:9]
        keys, values, flipped = rest[9:]

        @pl.when(pl.program_id(0) == 0)
        def _():
            acc_ref[...] = jnp.zeros_like(acc_ref)
            load_kv(kv_in, keys, values)
            flipped[...] = values[...].T
            total = sum(scalar_of(r[...].reshape(-1, 2 * HD)) for r in kv_in[:-1])
            sum_ref[...] = jnp.broadcast_to(total, sum_ref.shape)

        pre = sum(wide(r[0]) for r in q_in[:2]) + sum(wide(r[...]) for r in q_in[2:])
        mixing = sum(wide(r[0]) for r in m_in[:4]) + wide(m_in[4][...])
        stack = stack_heads(pre)
        pre_ref[...] = stack
        mixing_ref[...] = stack_heads(mixing)
        scale = lax.rsqrt(jnp.mean(stack * stack, axis=-1, keepdims=True) + norm_eps)
        cosine = jnp.concatenate([cos_ref[...]] * PAIR, axis=0)
        sine = jnp.concatenate([sin_ref[...]] * PAIR, axis=0)
        query = turn(stack * scale * gain_ref[...], cosine, sine).astype(BF)
        probs = probabilities(query, keys[...], rows)
        mixed = jnp.dot(flipped[...], probs.astype(BF), preferred_element_type=F32)
        mixed = lay_heads(mixed.T).astype(BF)
        query_ref[...] = query
        mixed_ref[...] = mixed
        terms = wide(mixed) * mixing
        acc_ref[...] += sum(terms[:, n * HD : (n + 1) * HD] for n in range(PAIR))

    heads = cols // HD
    wide_out = sds((heads * rows, HD), F32)
    low_out = sds((heads * rows, HD), BF)
    tall = pl.BlockSpec((PAIR * rows, HD), lambda h: (h, 0))
    return pl.pallas_call(
        kernel,
        grid=(cols // wide_cols,),
        in_specs=[stacked] * 2 + [flat] * 3 + [stacked] * 4 + [flat]
        + specs
        + [whole(v) for v in (cosine, sine, gain)],
        out_specs=[tall, tall, flat, tall]
        + [pl.BlockSpec((rows, HD), lambda h: (0, 0)), pl.BlockSpec((8, HD), lambda h: (0, 0))],
        out_shape=[wide_out, low_out, sds((rows, cols), BF), wide_out]
        + [sds((rows, HD), F32), sds((8, HD), F32)],
        scratch_shapes=[
            pltpu.VMEM((count, HD), BF),
            pltpu.VMEM((count, HD), BF),
            pltpu.VMEM((HD, count), BF),
        ],
        compiler_params=alone,
        cost_estimate=cost(8),
    )(*q_first, *q_rest, *m_pairs, m_last, *arrays, cosine, sine, gain)


def attention_slopes(pre, query, mixing, prompt, own_kv, cosine, sine, gain):
    rows = own_kv.shape[0]
    cols = query.shape[0] // rows * HD
    wide_cols = PAIR * HD
    count = KV_BLOCKS * rows
    tall = pl.BlockSpec((PAIR * rows, HD), lambda h: (h, 0))
    across = pl.BlockSpec((count, PAIR * rows), lambda h: (0, h))
    specs, arrays = kv_specs(prompt, own_kv)

    def kernel(pre_ref, query_ref, mixing_ref, *refs):
        kv_in, rest = refs[:KV_BLOCKS], refs[KV_BLOCKS:]
        cos_ref, sin_ref, gain_ref, probs_ref, score_ref, back_ref, keys, values, flipped = rest

        @pl.when(pl.program_id(0) == 0)
        def _():
            load_kv(kv_in, keys, values)
            flipped[...] = keys[...].T

        query = query_ref[...]
        probs = probabilities(query, keys[...], rows)
        probs_ref[...] = probs.astype(BF)
        grad = mixing_ref[...].astype(BF)
        prob_cot = lax.dot_general(values[...], grad, NT, preferred_element_type=F32)
        inner = jnp.sum(probs * prob_cot, axis=0, keepdims=True)
        score_cot = (probs * (prob_cot - inner) * HD ** (-0.5)).astype(BF)
        score_ref[...] = score_cot
        query_cot = jnp.dot(flipped[...], score_cot, preferred_element_type=F32).T
        cosine = jnp.concatenate([cos_ref[...]] * PAIR, axis=0)
        sine = jnp.concatenate([sin_ref[...]] * PAIR, axis=0)
        back_ref[...] = lay_heads(
            turn_back(pre_ref[...], gain_ref[...], cosine, sine, query_cot)
        )

    return pl.pallas_call(
        kernel,
        grid=(cols // wide_cols,),
        in_specs=[tall] * 3 + specs + [whole(v) for v in (cosine, sine, gain)],
        out_specs=[across, across, pl.BlockSpec((rows, wide_cols), lambda h: (0, h))],
        out_shape=[sds((count, query.shape[0]), BF)] * 2 + [sds((rows, cols), F32)],
        scratch_shapes=[
            pltpu.VMEM((count, HD), BF),
            pltpu.VMEM((count, HD), BF),
            pltpu.VMEM((HD, count), BF),
        ],
        compiler_params=alone,
        cost_estimate=cost(8),
    )(pre, query, mixing, *arrays, cosine, sine, gain)


def attention_back(slope, probs, score_cot, back, query, mixing, cosine, sine, k_pre, k_gain):
    rows, cols = back.shape
    heads = cols // HD
    own_cols = cols + 2 * HD
    send_cols = own_cols + 4 * HD
    count = KV_BLOCKS * rows

    def kernel(slope_ref, probs_ref, score_ref, back_ref, query_ref, mixing_ref, *refs):
        cos_ref, sin_ref, k_pre_ref, k_gain_ref, own_ref, home_ref, *send_refs = refs
        slope = slope_ref[...]
        tall = jnp.concatenate([slope] * heads, axis=0)
        query = (tall * wide(query_ref[...])).astype(BF)
        grad = (tall * mixing_ref[...]).astype(BF)
        key_cot = jnp.dot(score_ref[...], query, preferred_element_type=F32)
        value_cot = jnp.dot(probs_ref[...], grad, preferred_element_type=F32)
        cots = jnp.concatenate([key_cot.astype(BF), value_cot.astype(BF)], axis=1)

        def block(n):
            return cots[n * rows : (n + 1) * rows]

        own_k = turn_back(
            k_pre_ref[...], k_gain_ref[...], cos_ref[...], sin_ref[...], key_cot[count - rows :]
        )
        own = jnp.concatenate(
            [(slope * back_ref[...]).astype(BF), own_k.astype(BF), block(2 * XS)[:, HD:]], axis=1
        )
        own_ref[...] = own
        for n in range(2):
            home_ref[n] = block(n)
        for dx in range(1, XS):
            send_ref = send_refs[dx - 1]
            send_ref[:, :own_cols] = own
            for n in range(2):
                at = own_cols + n * 2 * HD
                send_ref[:, at : at + 2 * HD] = block(2 * (XS - dx) + n)

    send_out = sds((rows, send_cols), BF)
    outs = [sds((rows, own_cols), BF), sds((2, rows, 2 * HD), BF)] + [send_out] * (XS - 1)
    inputs = (slope, probs, score_cot, back, query, mixing, cosine, sine, k_pre, k_gain)
    return pl.pallas_call(
        kernel,
        grid=(1,),
        in_specs=[whole(v) for v in inputs],
        out_specs=[whole(v) for v in outs],
        out_shape=outs,
        compiler_params=alone,
        cost_estimate=cost(4),
    )(*inputs)


def weight_grad(left, blocks, cols, tile):
    def kernel(left_ref, *refs):
        right = jnp.concatenate(
            [r[...].reshape(-1, tile) for r in refs[:-1]], axis=0
        )
        refs[-1][...] = jnp.dot(left_ref[...], right, preferred_element_type=F32).astype(BF)

    specs = [
        pl.BlockSpec(b.shape[:-1] + (tile,), lambda c, n=b.ndim: (0,) * (n - 1) + (c,)) for b in blocks
    ]
    return pl.pallas_call(
        kernel,
        grid=(cols // tile,),
        in_specs=[whole(left)] + specs,
        out_specs=pl.BlockSpec((left.shape[0], tile), lambda c: (0, c)),
        out_shape=sds((left.shape[0], cols), BF),
        compiler_params=params,
        cost_estimate=cost(3),
    )(left, *blocks)


def weight_grad_kv(order, left_x, blocks, left_p, prompt, kcols):
    tile = 2 * kcols
    rows, cols = blocks[0].shape
    at = cols // tile - 1
    count = len(blocks)

    def kernel(order_ref, x_ref, p_ref, *refs):
        k_ref, v_ref, sum_ref = refs[-3:]
        right = jnp.concatenate([r[...] for r in refs[:count]], axis=0)
        total = jnp.dot(x_ref[...], right, preferred_element_type=F32)
        more = [r[...].reshape(-1, tile) for r in refs[count:-3]]
        right = jnp.concatenate([m[:rows] for m in more], axis=0)
        total += jnp.dot(p_ref[...], right, preferred_element_type=F32)
        k_ref[...] = total[:, :kcols].astype(BF)
        v_ref[...] = total[:, kcols:].astype(BF)
        scalars = [scalar_of(m) for m in more]
        added = jnp.zeros((1, 1), F32)
        for device in range(count):
            added += sum(jnp.where(order_ref[n] == device, scalars[n], 0.0) for n in range(count))
        sum_ref[...] = jnp.broadcast_to(added, sum_ref.shape)

    specs = [pl.BlockSpec((rows, tile), lambda c, o: (0, at))] * count
    for array, index in prompt:
        if index is None:
            specs.append(pl.BlockSpec((rows + TAIL, tile), lambda c, o: (0, 0)))
        else:
            specs.append(
                pl.BlockSpec((1, rows + TAIL, tile), lambda c, o, index=index: (index, 0, 0))
            )
    narrow = sds((left_x.shape[0], kcols), BF)
    outs = [narrow, narrow, sds((8, HD), F32)]
    return pl.pallas_call(
        kernel,
        grid_spec=pltpu.PrefetchScalarGridSpec(
            num_scalar_prefetch=1,
            grid=(1,),
            in_specs=[whole(left_x), whole(left_p)] + specs,
            out_specs=[whole(v) for v in outs],
        ),
        out_shape=outs,
        compiler_params=params,
        cost_estimate=cost(3),
    )(order, left_x, left_p, *blocks, *[array for array, _ in prompt])


def tables(positions):
    half = HD // 2
    frequency = jnp.exp(jnp.arange(half, dtype=F32) * (-2.0 * math.log(rope_base) / HD))
    angles = positions[:, None] * frequency[None, :]
    cosine, sine = jnp.cos(angles), jnp.sin(angles)
    return jnp.concatenate([cosine, cosine], axis=1), jnp.concatenate([-sine, sine], axis=1)


def body(
    resp_hidden,
    prompt_hidden,
    readout,
    query_weight,
    key_weight,
    value_weight,
    out_weight,
    query_gain,
    key_gain,
    base_logprob,
    behavior_logprob,
    reference_logprob,
    rewards,
    lengths,
):
    own_x = resp_hidden[0]
    own_read = readout[0]
    rows = own_x.shape[0]
    qcols = query_weight.shape[1]
    kcols = key_weight.shape[1]
    groups = lax.axis_size("resp")
    index = lax.axis_index("resp").astype(jnp.int32)
    offset = jnp.arange(2 * XS, dtype=jnp.int32)
    order = ((index // 2 + offset % XS) % XS) * 2 + (index % 2 + offset // XS) % 2

    packed, own_acc = pack(own_x, prompt_hidden, own_read)
    tokens = exchange(packed)
    own_part = jnp.sum(own_acc, axis=-1)
    prompt_pos = (index * rows + jnp.arange(rows)).astype(F32)
    resp_pos = (rows * groups + jnp.arange(rows)).astype(F32)
    prompt_cos, prompt_sin = tables(prompt_pos)
    resp_cos, resp_sin = tables(resp_pos)

    kv_weight = jnp.concatenate([key_weight, value_weight], axis=1)
    qkv_weight = jnp.concatenate([query_weight, kv_weight], axis=1)
    okv_weight = jnp.concatenate([out_weight, kv_weight], axis=1)
    tiles = qkv_weight.shape[1] // 256

    pairs = list(project(order, tokens, [2] * (tiles - 1) + [1], okv_weight, True))
    got_m = [send(pairs[n], n) for n in range(1, XS)]
    pairs[0], tokens = lax.optimization_barrier((pairs[0], tokens))
    near_q, far_q = project(order, tokens, [0] * tiles, qkv_weight, False)
    got_q = send(far_q, 0, 1)
    far_q, tokens = lax.optimization_barrier((far_q, tokens))
    flipped = flip_tokens(order, tokens)
    got_m, flipped = lax.optimization_barrier((got_m, flipped))
    left_x, left_p, left_r = flipped
    far_m = (wide(pairs[0][1]) + sum(wide(g[1]) for g in got_m)).astype(BF)
    last_m = send(far_m, 0, 1)
    half_q = [(wide(near_q[n]) + wide(got_q[n])).astype(BF) for n in range(1, XS)]
    parts_q = [send(half_q[n - 1], n) for n in range(1, XS)]
    kv_pre = wide(pairs[0][0, :, qcols:]) + sum(wide(g[0, :, qcols:]) for g in got_m)
    kv_pre = kv_pre + wide(last_m[:, qcols:])
    kp_pre = kv_pre[:, :kcols]
    prompt_keys = norm_rope(kp_pre, key_gain, prompt_pos)
    kv_block = jnp.concatenate([prompt_keys.astype(BF), kv_pre[:, kcols:].astype(BF)], axis=1)
    kv_block = with_scalar(kv_block, rewards[0])
    other_kv = send(kv_block, 0, 1)
    parts_q, kv_block, other_kv = lax.optimization_barrier((parts_q, kv_block, other_kv))
    pair_kv = jnp.stack([kv_block, other_kv])
    got_kv = [send(pair_kv, n) for n in range(1, XS)]
    kvr_pre = wide(near_q[0][:, qcols:]) + wide(got_q[0][:, qcols:])
    kvr_pre = kvr_pre + sum(wide(part[:, qcols:]) for part in parts_q)
    kr_pre = kvr_pre[:, :kcols]
    resp_keys = norm_rope(kr_pre, key_gain, resp_pos)
    own_kv = jnp.concatenate([resp_keys.astype(BF), kvr_pre[:, kcols:].astype(BF)], axis=1)
    prompt_kv = [kv_block, other_kv] + got_kv

    q_gain, k_gain = query_gain[None, :], key_gain[None, :]
    q_pre, query, mixed, mixing, attn_acc, reward_sum = attention(
        (near_q, got_q),
        parts_q,
        [pairs[0]] + got_m,
        last_m,
        prompt_kv,
        own_kv,
        resp_cos,
        resp_sin,
        q_gain,
    )
    probs, score_cot, back = attention_slopes(
        q_pre, query, mixing, prompt_kv, own_kv, resp_cos, resp_sin, q_gain
    )
    attn_logit = xor_sum(jnp.sum(attn_acc, axis=-1)[None, :], "head")[0]
    logprob = base_logprob[0] + own_part + attn_logit
    advantage = rewards[0] - reward_sum[0, 0] / groups
    live = (jnp.arange(rows) < lengths[0]).astype(F32)
    loss_own, lp_slope = objective(
        logprob, behavior_logprob[0], reference_logprob[0], advantage, live
    )
    mixing_grad = (lp_slope[:, None] * wide(mixed)).astype(BF)
    near_dm = [mixing_grad] + [send(mixing_grad, XS - n) for n in range(1, XS)]
    own_cots, home, *send_cots = attention_back(
        lp_slope[:, None],
        probs,
        score_cot,
        back,
        query,
        mixing,
        resp_cos,
        resp_sin,
        kr_pre,
        k_gain,
    )
    first_dm = send(mixing_grad, 0, 1)
    own_cots, home, send_cots, near_dm, first_dm = lax.optimization_barrier(
        (own_cots, home, send_cots, near_dm, first_dm)
    )
    got_d = [send(send_cots[n], n + 1) for n in range(XS - 1)]
    other_cots = send(own_cots, 0, 1)
    far_dm = send(jnp.stack(near_dm[1:]), 0, 1)
    got_d, other_cots, far_dm = lax.optimization_barrier((got_d, other_cots, far_dm))
    at = qcols + 2 * kcols
    far_kv = (wide(home[1]) + sum(wide(g[:, at + 2 * kcols :]) for g in got_d)).astype(BF)
    last_kv = send(far_kv, 0, 1)
    far_d = [send(other_cots, n) for n in range(1, XS)]
    dkv = wide(home[0]) + sum(wide(g[:, at : at + 2 * kcols]) for g in got_d) + wide(last_kv)
    dkp = turn_back(kp_pre, k_gain, prompt_cos, prompt_sin, dkv[:, :kcols])
    block_dp = jnp.concatenate([dkp.astype(BF), dkv[:, kcols:].astype(BF)], axis=1)
    block_dp = with_scalar(block_dp, loss_own)
    other_dp = send(block_dp, 0, 1)
    out_grad = weight_grad(left_r, near_dm + [first_dm, far_dm], qcols, 512)
    far_d, other_dp, out_grad = lax.optimization_barrier((far_d, other_dp, out_grad))
    pair_dp = jnp.stack([block_dp, other_dp])
    got_dp = [send(pair_dp, n) for n in range(1, XS)]
    by_offset = [2, 1, 0]
    cots = [own_cots] + [got_d[n] for n in by_offset]
    cots += [other_cots] + [far_d[n] for n in by_offset]
    query_grad = weight_grad(left_x, cots, qcols, 512)
    got_dp, query_grad = lax.optimization_barrier((got_dp, query_grad))
    prompt = [(block_dp, None)] + [(got_dp[n], 0) for n in by_offset]
    prompt += [(other_dp, None)] + [(got_dp[n], 1) for n in by_offset]
    key_grad, value_grad, loss = weight_grad_kv(order, left_x, cots, left_p, prompt, kcols)
    group_loss = loss[0, :1]
    return (
        logprob[None, :],
        group_loss,
        query_grad,
        key_grad,
        value_grad,
        out_grad,
    )


def solution(mesh):
    placed = (
        P(("grp", "resp"), None, None),
        P(("grp", "resp"), None),
        P(("grp", "resp"), None, None),
        P("resp", "head"),
        P("resp", "head"),
        P("resp", "head"),
        P("resp", "head"),
        P(),
        P(),
        P(("grp", "resp"), None),
        P(("grp", "resp"), None),
        P(("grp", "resp"), None),
        P(("grp", "resp")),
        P(("grp", "resp")),
    )
    return jax.shard_map(
        body,
        mesh=mesh,
        in_specs=placed,
        out_specs=(
            P(("grp", "resp"), None),
            P("grp"),
            P(("grp", "resp"), "head"),
            P(("grp", "resp"), "head"),
            P(("grp", "resp"), "head"),
            P(("grp", "resp"), "head"),
        ),
        check_vma=False,
    )
```

```python
import math

import jax
import jax.numpy as jnp
from jax import lax
from jax.experimental import pallas as pl
from jax.experimental.pallas import tpu as pltpu
from jax.sharding import PartitionSpec as P

HD = 128


norm_eps = 1e-06
rope_base = 1000000.0
clip_low = 0.8
clip_high = 1.28
kl_weight = 0.04


def objective(logprob, behavior, reference_lp, advantage, live):
    ratios = jnp.exp(logprob - behavior)
    weight = jnp.clip(ratios, clip_low, clip_high)
    ref_gap = reference_lp - logprob
    penalty = jnp.exp(ref_gap) - ref_gap - 1.0
    token_loss = live * (kl_weight * penalty - weight * advantage * logprob)
    lp_slope = live * (kl_weight * (1.0 - jnp.exp(ref_gap)) - weight * advantage)
    return (jnp.sum(token_loss), lp_slope)


XS = 4
BF = jnp.bfloat16
F32 = jnp.float32
NT = (((1,), (1,)), ((), ()))
TN = (((0,), (0,)), ((), ()))
PAIR = 4
params = pltpu.CompilerParams(vmem_limit_bytes=30 * 1024 * 1024)
alone = pltpu.CompilerParams(vmem_limit_bytes=60 * 1024 * 1024)


TAIL = 16


def cost(us):
    return pl.CostEstimate(flops=int(us * 1e8), bytes_accessed=1 << 18, transcendentals=0)


def wide(value):
    return value.astype(F32)


def sds(shape, dtype):
    return jax.ShapeDtypeStruct(shape, dtype)


def whole(array):
    shape = array.shape
    return pl.BlockSpec(shape, lambda *_: (0,) * len(shape))


def send(value, dx, dy=0):
    pairs = [(x * 2 + y, ((x + dx) % XS) * 2 + (y ^ dy)) for x in range(XS) for y in range(2)]
    return lax.ppermute(value, "resp", pairs)


def xor_sum(value, axis):
    def flip(term, step):
        return lax.ppermute(term, axis, [(i, i ^ step) for i in range(2 * XS)])

    quad = (value + flip(value, 1)) + (flip(value, 2) + flip(value, 3))
    return quad + flip(quad, 4)


def with_scalar(block, scalar):
    high = lax.reduce_precision(scalar, 8, 7)
    rest = scalar - high
    middle = lax.reduce_precision(rest, 8, 7)
    terms = jnp.stack([high, middle, rest - middle]).astype(BF)
    tail = jnp.zeros((TAIL, block.shape[1]), BF).at[0, :3].set(terms)
    return jnp.concatenate([block, tail], axis=0)


def scalar_of(block):
    return jnp.sum(jnp.sum(wide(block[-TAIL:]), axis=0, keepdims=True), axis=1, keepdims=True)


def exchange(blocks):
    return lax.all_to_all(blocks, "resp", split_axis=0, concat_axis=0, tiled=True)


def pack(own_x, own_p, own_r):
    rows, depth = own_x.shape
    width = depth // (2 * XS)

    def kernel(x_ref, p_ref, r_ref, out_ref, acc_ref):
        x, r = x_ref[...], r_ref[...]
        for n in range(2):
            at = slice(n * width, (n + 1) * width)
            out_ref[n, :rows] = x[:, at]
            out_ref[n, rows : 2 * rows] = p_ref[:, at]
            out_ref[n, 2 * rows :] = r[:, at]
        terms = wide(x) * wide(r)
        total = sum(terms[:, n : n + HD] for n in range(0, 2 * width, HD))

        @pl.when(pl.program_id(0) == 0)
        def _():
            acc_ref[...] = total

        @pl.when(pl.program_id(0) > 0)
        def _():
            acc_ref[...] += total

    return pl.pallas_call(
        kernel,
        grid=(XS,),
        out_shape=[sds((2 * XS, 3 * rows, width), BF), sds((rows, HD), F32)],
        in_specs=[pl.BlockSpec((rows, 2 * width), lambda n: (0, n))] * 3,
        out_specs=[
            pl.BlockSpec((2, 3 * rows, width), lambda n: (n, 0, 0)),
            pl.BlockSpec((rows, HD), lambda n: (0, 0)),
        ],
        compiler_params=alone,
        cost_estimate=cost(4),
    )(own_x, own_p, own_r)


def project(blocks, weight):
    got = jnp.einsum("ntd,dc->ntc", blocks, weight, preferred_element_type=F32).astype(BF)
    return got.reshape((XS, 2) + got.shape[1:])


def pick(array, index, axis=0):
    return lax.dynamic_index_in_dim(array, index, axis, keepdims=False)


def flip_tokens(order, tokens):
    width = tokens.shape[2]
    rows = tokens.shape[1] // 3

    def kernel(order_ref, tokens_ref, x_ref, p_ref, r_ref):
        x_ref[...] = tokens_ref[0, :rows].T
        p_ref[...] = tokens_ref[0, rows : 2 * rows].T
        r_ref[...] = tokens_ref[0, 2 * rows :].T

    by_offset = pl.BlockSpec((width, rows), lambda s, o: (0, s))
    return pl.pallas_call(
        kernel,
        grid_spec=pltpu.PrefetchScalarGridSpec(
            num_scalar_prefetch=1,
            grid=(2 * XS,),
            in_specs=[pl.BlockSpec((1, 3 * rows, width), lambda s, o: (o[s], 0, 0))],
            out_specs=[by_offset] * 3,
        ),
        out_shape=[sds((width, 2 * XS * rows), BF)] * 3,
        compiler_params=params,
        cost_estimate=cost(8),
    )(order, tokens)


KV_BLOCKS = 2 * XS + 1


def kv_specs(prompt, own_kv):
    rows = own_kv.shape[0] + TAIL
    specs = [pl.BlockSpec((rows, 2 * HD), lambda h: (0, 0))] * 2
    arrays = list(prompt[:2])
    for array in prompt[2:]:
        for n in range(2):
            specs.append(pl.BlockSpec((1, rows, 2 * HD), lambda h, n=n: (n, 0, 0)))
            arrays.append(array)
    return specs + [whole(own_kv)], arrays + [own_kv]


def load_kv(refs, keys, values):
    rows = refs[-1].shape[0]
    for n, ref in enumerate(refs):
        block = ref[...].reshape(-1, 2 * HD)[:rows]
        keys[n * rows : (n + 1) * rows] = block[:, :HD]
        values[n * rows : (n + 1) * rows] = block[:, HD:]


def probabilities(query, keys, rows):
    scores = lax.dot_general(keys, query, NT, preferred_element_type=F32) * HD ** (-0.5)
    weights = jnp.exp(scores)
    key = lax.broadcasted_iota(jnp.int32, (rows, query.shape[0]), 0)
    position = lax.broadcasted_iota(jnp.int32, (rows, query.shape[0]), 1) % rows
    count = keys.shape[0] - rows
    own = jnp.where(key <= position, weights[count:], 0.0)
    weights = jnp.concatenate([weights[:count], own], axis=0)
    return weights * (1.0 / jnp.sum(weights, axis=0, keepdims=True))


def stack_heads(value):
    return jnp.concatenate([value[:, n * HD : (n + 1) * HD] for n in range(PAIR)], axis=0)


def lay_heads(value):
    rows = value.shape[0] // PAIR
    return jnp.concatenate([value[n * rows : (n + 1) * rows] for n in range(PAIR)], axis=1)


def turn(normed, cosine, sine):
    return normed * cosine + pltpu.roll(normed, HD // 2, 1) * sine


def turn_rows(pre, gain, cosine, sine):
    half = HD // 2
    normed = pre * lax.rsqrt(jnp.mean(pre * pre, axis=-1, keepdims=True) + norm_eps) * gain
    flipped = jnp.concatenate([normed[:, half:], normed[:, :half]], axis=1)
    return normed * cosine + flipped * sine


def turn_back(pre, gain, cosine, sine, cotangent):
    scale = lax.rsqrt(jnp.mean(pre * pre, axis=-1, keepdims=True) + norm_eps)
    half = HD // 2
    flipped = jnp.concatenate([cotangent[:, half:], cotangent[:, :half]], axis=1)
    inner = (cotangent * cosine - flipped * sine) * gain
    return scale * inner - pre * (scale * scale * scale * jnp.mean(pre * inner, axis=-1, keepdims=True))


def attention(q_first, q_rest, mix, prompt, own_kv, cosine, sine, gain):
    rows, cols = mix.shape[0], mix.shape[1] - 2 * HD
    wide_cols = PAIR * HD
    count = KV_BLOCKS * rows
    specs, arrays = kv_specs(prompt, own_kv)
    flat = pl.BlockSpec((rows, wide_cols), lambda h: (0, h))

    def kernel(*refs):
        q_in, m_in, rest = refs[:4], refs[4], refs[5:]
        kv_in, rest = rest[:KV_BLOCKS], rest[KV_BLOCKS:]
        cos_ref, sin_ref, gain_ref = rest[:3]
        pre_ref, query_ref, mixed_ref, mixing_ref, acc_ref, sum_ref = rest[3:9]
        keys, values, flipped = rest[9:]

        @pl.when(pl.program_id(0) == 0)
        def _():
            acc_ref[...] = jnp.zeros_like(acc_ref)
            load_kv(kv_in, keys, values)
            flipped[...] = values[...].T
            total = sum(scalar_of(r[...].reshape(-1, 2 * HD)) for r in kv_in[:-1])
            sum_ref[...] = jnp.broadcast_to(total, sum_ref.shape)

        pre = sum(wide(r[...]) for r in q_in)
        mixing = m_in[...]
        stack = stack_heads(pre)
        pre_ref[...] = stack
        mixing_ref[...] = stack_heads(mixing)
        scale = lax.rsqrt(jnp.mean(stack * stack, axis=-1, keepdims=True) + norm_eps)
        cosine = jnp.concatenate([cos_ref[...]] * PAIR, axis=0)
        sine = jnp.concatenate([sin_ref[...]] * PAIR, axis=0)
        query = turn(stack * scale * gain_ref[...], cosine, sine).astype(BF)
        probs = probabilities(query, keys[...], rows)
        mixed = jnp.dot(flipped[...], probs.astype(BF), preferred_element_type=F32)
        mixed = lay_heads(mixed.T).astype(BF)
        query_ref[...] = query
        mixed_ref[...] = mixed
        terms = wide(mixed) * mixing
        acc_ref[...] += sum(terms[:, n * HD : (n + 1) * HD] for n in range(PAIR))

    heads = cols // HD
    wide_out = sds((heads * rows, HD), F32)
    low_out = sds((heads * rows, HD), BF)
    tall = pl.BlockSpec((PAIR * rows, HD), lambda h: (h, 0))
    return pl.pallas_call(
        kernel,
        grid=(cols // wide_cols,),
        in_specs=[flat] * 5
        + specs
        + [whole(v) for v in (cosine, sine, gain)],
        out_specs=[tall, tall, flat, tall]
        + [pl.BlockSpec((rows, HD), lambda h: (0, 0)), pl.BlockSpec((8, HD), lambda h: (0, 0))],
        out_shape=[wide_out, low_out, sds((rows, cols), BF), wide_out]
        + [sds((rows, HD), F32), sds((8, HD), F32)],
        scratch_shapes=[
            pltpu.VMEM((count, HD), BF),
            pltpu.VMEM((count, HD), BF),
            pltpu.VMEM((HD, count), BF),
        ],
        compiler_params=alone,
        cost_estimate=cost(8),
    )(q_first, *q_rest, mix, *arrays, cosine, sine, gain)


def attention_slopes(pre, query, mixing, prompt, own_kv, cosine, sine, gain):
    rows = own_kv.shape[0]
    cols = query.shape[0] // rows * HD
    wide_cols = PAIR * HD
    count = KV_BLOCKS * rows
    tall = pl.BlockSpec((PAIR * rows, HD), lambda h: (h, 0))
    across = pl.BlockSpec((count, PAIR * rows), lambda h: (0, h))
    specs, arrays = kv_specs(prompt, own_kv)

    def kernel(pre_ref, query_ref, mixing_ref, *refs):
        kv_in, rest = refs[:KV_BLOCKS], refs[KV_BLOCKS:]
        cos_ref, sin_ref, gain_ref, probs_ref, score_ref, back_ref, keys, values, flipped = rest

        @pl.when(pl.program_id(0) == 0)
        def _():
            load_kv(kv_in, keys, values)
            flipped[...] = keys[...].T

        query = query_ref[...]
        probs = probabilities(query, keys[...], rows)
        probs_ref[...] = probs.astype(BF)
        grad = mixing_ref[...].astype(BF)
        prob_cot = lax.dot_general(values[...], grad, NT, preferred_element_type=F32)
        inner = jnp.sum(probs * prob_cot, axis=0, keepdims=True)
        score_cot = (probs * (prob_cot - inner) * HD ** (-0.5)).astype(BF)
        score_ref[...] = score_cot
        query_cot = jnp.dot(flipped[...], score_cot, preferred_element_type=F32).T
        cosine = jnp.concatenate([cos_ref[...]] * PAIR, axis=0)
        sine = jnp.concatenate([sin_ref[...]] * PAIR, axis=0)
        back_ref[...] = lay_heads(
            turn_back(pre_ref[...], gain_ref[...], cosine, sine, query_cot)
        )

    return pl.pallas_call(
        kernel,
        grid=(cols // wide_cols,),
        in_specs=[tall] * 3 + specs + [whole(v) for v in (cosine, sine, gain)],
        out_specs=[across, across, pl.BlockSpec((rows, wide_cols), lambda h: (0, h))],
        out_shape=[sds((count, query.shape[0]), BF)] * 2 + [sds((rows, cols), F32)],
        scratch_shapes=[
            pltpu.VMEM((count, HD), BF),
            pltpu.VMEM((count, HD), BF),
            pltpu.VMEM((HD, count), BF),
        ],
        compiler_params=alone,
        cost_estimate=cost(8),
    )(pre, query, mixing, *arrays, cosine, sine, gain)


def attention_back(slope, probs, score_cot, back, query, mixing, cosine, sine, k_pre, k_gain):
    rows, cols = back.shape
    heads = cols // HD
    own_cols = cols + 2 * HD
    send_cols = own_cols + 4 * HD
    count = KV_BLOCKS * rows

    def kernel(slope_ref, probs_ref, score_ref, back_ref, query_ref, mixing_ref, *refs):
        cos_ref, sin_ref, k_pre_ref, k_gain_ref, own_ref, home_ref, *send_refs = refs
        slope = slope_ref[...]
        tall = jnp.concatenate([slope] * heads, axis=0)
        query = (tall * wide(query_ref[...])).astype(BF)
        grad = (tall * mixing_ref[...]).astype(BF)
        key_cot = jnp.dot(score_ref[...], query, preferred_element_type=F32)
        value_cot = jnp.dot(probs_ref[...], grad, preferred_element_type=F32)
        cots = jnp.concatenate([key_cot.astype(BF), value_cot.astype(BF)], axis=1)

        def block(n):
            return cots[n * rows : (n + 1) * rows]

        own_k = turn_back(
            k_pre_ref[...], k_gain_ref[...], cos_ref[...], sin_ref[...], key_cot[count - rows :]
        )
        own = jnp.concatenate(
            [(slope * back_ref[...]).astype(BF), own_k.astype(BF), block(2 * XS)[:, HD:]], axis=1
        )
        own_ref[...] = own
        for n in range(2):
            home_ref[n] = block(n)
        for dx in range(1, XS):
            send_ref = send_refs[dx - 1]
            send_ref[:, :own_cols] = own
            for n in range(2):
                at = own_cols + n * 2 * HD
                send_ref[:, at : at + 2 * HD] = block(2 * (XS - dx) + n)

    send_out = sds((rows, send_cols), BF)
    outs = [sds((rows, own_cols), BF), sds((2, rows, 2 * HD), BF)] + [send_out] * (XS - 1)
    inputs = (slope, probs, score_cot, back, query, mixing, cosine, sine, k_pre, k_gain)
    return pl.pallas_call(
        kernel,
        grid=(1,),
        in_specs=[whole(v) for v in inputs],
        out_specs=[whole(v) for v in outs],
        out_shape=outs,
        compiler_params=alone,
        cost_estimate=cost(4),
    )(*inputs)


def weight_grad(left, blocks, cols, tile):
    def kernel(left_ref, *refs):
        right = jnp.concatenate(
            [r[...].reshape(-1, tile) for r in refs[:-1]], axis=0
        )
        refs[-1][...] = jnp.dot(left_ref[...], right, preferred_element_type=F32).astype(BF)

    specs = [
        pl.BlockSpec(b.shape[:-1] + (tile,), lambda c, n=b.ndim: (0,) * (n - 1) + (c,)) for b in blocks
    ]
    return pl.pallas_call(
        kernel,
        grid=(cols // tile,),
        in_specs=[whole(left)] + specs,
        out_specs=pl.BlockSpec((left.shape[0], tile), lambda c: (0, c)),
        out_shape=sds((left.shape[0], cols), BF),
        compiler_params=params,
        cost_estimate=cost(3),
    )(left, *blocks)


def weight_grad_kv(order, left_x, blocks, left_p, prompt, kcols):
    tile = 2 * kcols
    rows, cols = blocks[0].shape
    at = cols // tile - 1
    count = len(blocks)

    def kernel(order_ref, x_ref, p_ref, *refs):
        k_ref, v_ref, sum_ref = refs[-3:]
        right = jnp.concatenate([r[...] for r in refs[:count]], axis=0)
        total = jnp.dot(x_ref[...], right, preferred_element_type=F32)
        more = [r[...].reshape(-1, tile) for r in refs[count:-3]]
        right = jnp.concatenate([m[:rows] for m in more], axis=0)
        total += jnp.dot(p_ref[...], right, preferred_element_type=F32)
        k_ref[...] = total[:, :kcols].astype(BF)
        v_ref[...] = total[:, kcols:].astype(BF)
        scalars = [scalar_of(m) for m in more]
        added = jnp.zeros((1, 1), F32)
        for device in range(count):
            added += sum(jnp.where(order_ref[n] == device, scalars[n], 0.0) for n in range(count))
        sum_ref[...] = jnp.broadcast_to(added, sum_ref.shape)

    specs = [pl.BlockSpec((rows, tile), lambda c, o: (0, at))] * count
    for array, index in prompt:
        if index is None:
            specs.append(pl.BlockSpec((rows + TAIL, tile), lambda c, o: (0, 0)))
        else:
            specs.append(
                pl.BlockSpec((1, rows + TAIL, tile), lambda c, o, index=index: (index, 0, 0))
            )
    narrow = sds((left_x.shape[0], kcols), BF)
    outs = [narrow, narrow, sds((8, HD), F32)]
    return pl.pallas_call(
        kernel,
        grid_spec=pltpu.PrefetchScalarGridSpec(
            num_scalar_prefetch=1,
            grid=(1,),
            in_specs=[whole(left_x), whole(left_p)] + specs,
            out_specs=[whole(v) for v in outs],
        ),
        out_shape=outs,
        compiler_params=params,
        cost_estimate=cost(3),
    )(order, left_x, left_p, *blocks, *[array for array, _ in prompt])


def tables(positions):
    half = HD // 2
    frequency = jnp.exp(jnp.arange(half, dtype=F32) * (-2.0 * math.log(rope_base) / HD))
    angles = positions[:, None] * frequency[None, :]
    cosine, sine = jnp.cos(angles), jnp.sin(angles)
    return jnp.concatenate([cosine, cosine], axis=1), jnp.concatenate([-sine, sine], axis=1)


def body(
    resp_hidden,
    prompt_hidden,
    readout,
    query_weight,
    key_weight,
    value_weight,
    out_weight,
    query_gain,
    key_gain,
    base_logprob,
    behavior_logprob,
    reference_logprob,
    rewards,
    lengths,
):
    own_x = resp_hidden[0]
    own_read = readout[0]
    rows = own_x.shape[0]
    qcols = query_weight.shape[1]
    kcols = key_weight.shape[1]
    groups = lax.axis_size("resp")
    index = lax.axis_index("resp").astype(jnp.int32)
    offset = jnp.arange(2 * XS, dtype=jnp.int32)
    order = ((index // 2 + offset % XS) % XS) * 2 + (index % 2 + offset // XS) % 2

    packed, own_acc = pack(own_x, prompt_hidden, own_read)
    tokens = exchange(packed)
    own_part = jnp.sum(own_acc, axis=-1)
    prompt_pos = (index * rows + jnp.arange(rows)).astype(F32)
    resp_pos = (rows * groups + jnp.arange(rows)).astype(F32)
    prompt_cos, prompt_sin = tables(prompt_pos)
    resp_cos, resp_sin = tables(resp_pos)

    kv_weight = jnp.concatenate([key_weight, value_weight], axis=1)
    qkv_weight = jnp.concatenate([query_weight, kv_weight], axis=1)
    at_x, at_y = index // 2, index % 2

    ready = (own_part, prompt_cos, prompt_sin, resp_cos, resp_sin, kv_weight, qkv_weight)
    ready, tokens = lax.optimization_barrier((ready, tokens))
    own_part, prompt_cos, prompt_sin, resp_cos, resp_sin, kv_weight, qkv_weight = ready

    q_parts = project(tokens[:, :rows], qkv_weight)
    far_q = pick(q_parts, 1 - at_y, 1)
    got_q = send(far_q, 0, 1)
    far_q, tokens = lax.optimization_barrier((far_q, tokens))
    m_parts = project(tokens[:, 2 * rows :], out_weight)
    kv_parts = project(tokens[:, rows : 2 * rows], kv_weight)
    pairs = []
    for n in range(XS):
        to = (at_x + n) % XS
        pairs.append(jnp.concatenate([pick(m_parts, to), pick(kv_parts, to)], axis=2))
    got_m = [send(pairs[n], n) for n in range(1, XS)]
    pairs, tokens = lax.optimization_barrier((pairs, tokens))
    flipped = flip_tokens(order, tokens)
    got_q, flipped = lax.optimization_barrier((got_q, flipped))
    left_x, left_p, left_r = flipped

    def half(n):
        to = (at_x + n) % XS
        return wide(pick(pick(q_parts, to), at_y)) + wide(pick(got_q, to))

    half_q = [half(n).astype(BF) for n in range(1, XS)]
    parts_q = [send(half_q[n - 1], n) for n in range(1, XS)]
    got_m, half_q = lax.optimization_barrier((got_m, half_q))
    every_m = [pairs[0]] + got_m
    far_m = sum(wide(pick(g, 1 - at_y)) for g in every_m).astype(BF)
    last_m = send(far_m, 0, 1)
    mix = sum(wide(pick(g, at_y)) for g in every_m) + wide(last_m)
    kv_pre = mix[:, qcols:]
    kp_pre = kv_pre[:, :kcols]
    prompt_keys = turn_rows(kp_pre, key_gain, prompt_cos, prompt_sin)
    kv_block = jnp.concatenate([prompt_keys.astype(BF), kv_pre[:, kcols:].astype(BF)], axis=1)
    kv_block = with_scalar(kv_block, rewards[0])
    other_kv = send(kv_block, 0, 1)
    parts_q, kv_block, other_kv = lax.optimization_barrier((parts_q, kv_block, other_kv))
    pair_kv = jnp.stack([kv_block, other_kv])
    got_kv = [send(pair_kv, n) for n in range(1, XS)]
    first_q = half(0)
    kvr_pre = first_q[:, qcols:] + sum(wide(part[:, qcols:]) for part in parts_q)
    kr_pre = kvr_pre[:, :kcols]
    resp_keys = turn_rows(kr_pre, key_gain, resp_cos, resp_sin)
    own_kv = jnp.concatenate([resp_keys.astype(BF), kvr_pre[:, kcols:].astype(BF)], axis=1)
    prompt_kv = [kv_block, other_kv] + got_kv

    q_gain, k_gain = query_gain[None, :], key_gain[None, :]
    q_pre, query, mixed, mixing, attn_acc, reward_sum = attention(
        first_q,
        parts_q,
        mix,
        prompt_kv,
        own_kv,
        resp_cos,
        resp_sin,
        q_gain,
    )
    probs, score_cot, back = attention_slopes(
        q_pre, query, mixing, prompt_kv, own_kv, resp_cos, resp_sin, q_gain
    )
    attn_logit = xor_sum(jnp.sum(attn_acc, axis=-1)[None, :], "head")[0]
    attn_logit, probs, score_cot, back = lax.optimization_barrier(
        (attn_logit, probs, score_cot, back)
    )
    logprob = base_logprob[0] + own_part + attn_logit
    advantage = rewards[0] - reward_sum[0, 0] / groups
    live = (jnp.arange(rows) < lengths[0]).astype(F32)
    loss_own, lp_slope = objective(
        logprob, behavior_logprob[0], reference_logprob[0], advantage, live
    )
    mixing_grad = (lp_slope[:, None] * wide(mixed)).astype(BF)
    near_dm = [mixing_grad] + [send(mixing_grad, XS - n) for n in range(1, XS)]
    own_cots, home, *send_cots = attention_back(
        lp_slope[:, None],
        probs,
        score_cot,
        back,
        query,
        mixing,
        resp_cos,
        resp_sin,
        kr_pre,
        k_gain,
    )
    first_dm = send(mixing_grad, 0, 1)
    own_cots, home, send_cots, near_dm, first_dm = lax.optimization_barrier(
        (own_cots, home, send_cots, near_dm, first_dm)
    )
    got_d = [send(send_cots[n], n + 1) for n in range(XS - 1)]
    other_cots = send(own_cots, 0, 1)
    far_dm = send(jnp.stack(near_dm[1:]), 0, 1)
    got_d, other_cots, far_dm = lax.optimization_barrier((got_d, other_cots, far_dm))
    at = qcols + 2 * kcols
    far_kv = (wide(home[1]) + sum(wide(g[:, at + 2 * kcols :]) for g in got_d)).astype(BF)
    last_kv = send(far_kv, 0, 1)
    far_d = [send(other_cots, n) for n in range(1, XS)]
    dkv = wide(home[0]) + sum(wide(g[:, at : at + 2 * kcols]) for g in got_d) + wide(last_kv)
    dkp = turn_back(kp_pre, k_gain, prompt_cos, prompt_sin, dkv[:, :kcols])
    block_dp = jnp.concatenate([dkp.astype(BF), dkv[:, kcols:].astype(BF)], axis=1)
    block_dp = with_scalar(block_dp, loss_own)
    other_dp = send(block_dp, 0, 1)
    out_grad = weight_grad(left_r, near_dm + [first_dm, far_dm], qcols, 512)
    far_d, other_dp, out_grad = lax.optimization_barrier((far_d, other_dp, out_grad))
    pair_dp = jnp.stack([block_dp, other_dp])
    got_dp = [send(pair_dp, n) for n in range(1, XS)]
    by_offset = [2, 1, 0]
    cots = [own_cots] + [got_d[n] for n in by_offset]
    cots += [other_cots] + [far_d[n] for n in by_offset]
    query_grad = weight_grad(left_x, cots, qcols, 512)
    got_dp, query_grad = lax.optimization_barrier((got_dp, query_grad))
    prompt = [(block_dp, None)] + [(got_dp[n], 0) for n in by_offset]
    prompt += [(other_dp, None)] + [(got_dp[n], 1) for n in by_offset]
    key_grad, value_grad, loss = weight_grad_kv(order, left_x, cots, left_p, prompt, kcols)
    group_loss = loss[0, :1]
    return (
        logprob[None, :],
        group_loss,
        query_grad,
        key_grad,
        value_grad,
        out_grad,
    )


def solution(mesh):
    placed = (
        P(("grp", "resp"), None, None),
        P(("grp", "resp"), None),
        P(("grp", "resp"), None, None),
        P("resp", "head"),
        P("resp", "head"),
        P("resp", "head"),
        P("resp", "head"),
        P(),
        P(),
        P(("grp", "resp"), None),
        P(("grp", "resp"), None),
        P(("grp", "resp"), None),
        P(("grp", "resp")),
        P(("grp", "resp")),
    )
    return jax.shard_map(
        body,
        mesh=mesh,
        in_specs=placed,
        out_specs=(
            P(("grp", "resp"), None),
            P("grp"),
            P(("grp", "resp"), "head"),
            P(("grp", "resp"), "head"),
            P(("grp", "resp"), "head"),
            P(("grp", "resp"), "head"),
        ),
        check_vma=False,
    )
```

```python
import math

import jax
import jax.numpy as jnp
from jax import lax
from jax.experimental import pallas as pl
from jax.experimental.pallas import tpu as pltpu
from jax.sharding import PartitionSpec as P

HD = 128


norm_eps = 1e-06
rope_base = 1000000.0
clip_low = 0.8
clip_high = 1.28
kl_weight = 0.04


def objective(logprob, behavior, reference_lp, advantage, live):
    ratios = jnp.exp(logprob - behavior)
    weight = jnp.clip(ratios, clip_low, clip_high)
    ref_gap = reference_lp - logprob
    penalty = jnp.exp(ref_gap) - ref_gap - 1.0
    token_loss = live * (kl_weight * penalty - weight * advantage * logprob)
    lp_slope = live * (kl_weight * (1.0 - jnp.exp(ref_gap)) - weight * advantage)
    return (jnp.sum(token_loss), lp_slope)


XS = 4
BF = jnp.bfloat16
F32 = jnp.float32
NT = (((1,), (1,)), ((), ()))
TN = (((0,), (0,)), ((), ()))
PAIR = 4
params = pltpu.CompilerParams(vmem_limit_bytes=30 * 1024 * 1024)
alone = pltpu.CompilerParams(vmem_limit_bytes=60 * 1024 * 1024)


TAIL = 16


def cost(us):
    return pl.CostEstimate(flops=int(us * 1e8), bytes_accessed=1 << 18, transcendentals=0)


def wide(value):
    return value.astype(F32)


def sds(shape, dtype):
    return jax.ShapeDtypeStruct(shape, dtype)


def whole(array):
    shape = array.shape
    return pl.BlockSpec(shape, lambda *_: (0,) * len(shape))


def send(value, dx, dy=0):
    pairs = [(x * 2 + y, ((x + dx) % XS) * 2 + (y ^ dy)) for x in range(XS) for y in range(2)]
    return lax.ppermute(value, "resp", pairs)


def xor_sum(value, axis):
    def flip(term, step):
        return lax.ppermute(term, axis, [(i, i ^ step) for i in range(2 * XS)])

    quad = (value + flip(value, 1)) + (flip(value, 2) + flip(value, 3))
    return quad + flip(quad, 4)


def with_scalar(block, scalar):
    high = lax.reduce_precision(scalar, 8, 7)
    rest = scalar - high
    middle = lax.reduce_precision(rest, 8, 7)
    terms = jnp.stack([high, middle, rest - middle]).astype(BF)
    tail = jnp.zeros((TAIL, block.shape[1]), BF).at[0, :3].set(terms)
    return jnp.concatenate([block, tail], axis=0)


def scalar_of(block):
    return jnp.sum(jnp.sum(wide(block[-TAIL:]), axis=0, keepdims=True), axis=1, keepdims=True)


def exchange(blocks):
    return lax.all_to_all(blocks, "resp", split_axis=0, concat_axis=0, tiled=True)


def pack(*parts):
    rows, depth = parts[0].shape
    width = depth // (2 * XS)
    count = len(parts)

    def kernel(*refs):
        for part, ref in enumerate(refs[:count]):
            value = ref[...]
            for n in range(2):
                refs[count][n, part * rows : (part + 1) * rows] = value[:, n * width : (n + 1) * width]

    return pl.pallas_call(
        kernel,
        grid=(XS,),
        out_shape=sds((2 * XS, count * rows, width), BF),
        in_specs=[pl.BlockSpec((rows, 2 * width), lambda n: (0, n))] * count,
        out_specs=pl.BlockSpec((2, count * rows, width), lambda n: (n, 0, 0)),
        compiler_params=alone,
        cost_estimate=cost(2 * count),
    )(*parts)


def project(blocks, weight):
    got = jnp.einsum("ntd,dc->ntc", blocks, weight, preferred_element_type=F32).astype(BF)
    return got.reshape((XS, 2) + got.shape[1:])


def pick(array, index, axis=0):
    return lax.dynamic_index_in_dim(array, index, axis, keepdims=False)


def flip_tokens(order, tokens_x, tokens):
    width = tokens.shape[2]
    rows = tokens.shape[1] // 2

    def kernel(order_ref, own_ref, tokens_ref, x_ref, p_ref, r_ref):
        x_ref[...] = own_ref[0].T
        p_ref[...] = tokens_ref[0, :rows].T
        r_ref[...] = tokens_ref[0, rows:].T

    return pl.pallas_call(
        kernel,
        grid_spec=pltpu.PrefetchScalarGridSpec(
            num_scalar_prefetch=1,
            grid=(2 * XS,),
            in_specs=[
                pl.BlockSpec((1, rows, width), lambda s, o: (o[s], 0, 0)),
                pl.BlockSpec((1, 2 * rows, width), lambda s, o: (o[s], 0, 0)),
            ],
            out_specs=[pl.BlockSpec((width, rows), lambda s, o: (0, s))] * 3,
        ),
        out_shape=[sds((width, 2 * XS * rows), BF)] * 3,
        compiler_params=params,
        cost_estimate=cost(8),
    )(order, tokens_x, tokens)


KV_BLOCKS = 2 * XS + 1


def kv_specs(prompt, own_kv):
    rows = own_kv.shape[0] + TAIL
    specs = [pl.BlockSpec((rows, 2 * HD), lambda h: (0, 0))] * 2
    arrays = list(prompt[:2])
    for array in prompt[2:]:
        for n in range(2):
            specs.append(pl.BlockSpec((1, rows, 2 * HD), lambda h, n=n: (n, 0, 0)))
            arrays.append(array)
    return specs + [whole(own_kv)], arrays + [own_kv]


def load_kv(refs, keys, values):
    rows = refs[-1].shape[0]
    for n, ref in enumerate(refs):
        block = ref[...].reshape(-1, 2 * HD)[:rows]
        keys[n * rows : (n + 1) * rows] = block[:, :HD]
        values[n * rows : (n + 1) * rows] = block[:, HD:]


def probabilities(query, keys, rows):
    scores = lax.dot_general(keys, query, NT, preferred_element_type=F32) * HD ** (-0.5)
    weights = jnp.exp(scores)
    key = lax.broadcasted_iota(jnp.int32, (rows, query.shape[0]), 0)
    position = lax.broadcasted_iota(jnp.int32, (rows, query.shape[0]), 1) % rows
    count = keys.shape[0] - rows
    own = jnp.where(key <= position, weights[count:], 0.0)
    weights = jnp.concatenate([weights[:count], own], axis=0)
    return weights * (1.0 / jnp.sum(weights, axis=0, keepdims=True))


def stack_heads(value):
    return jnp.concatenate([value[:, n * HD : (n + 1) * HD] for n in range(PAIR)], axis=0)


def lay_heads(value):
    rows = value.shape[0] // PAIR
    return jnp.concatenate([value[n * rows : (n + 1) * rows] for n in range(PAIR)], axis=1)


def turn(normed, cosine, sine):
    return normed * cosine + pltpu.roll(normed, HD // 2, 1) * sine


def turn_rows(pre, gain, cosine, sine):
    half = HD // 2
    normed = pre * lax.rsqrt(jnp.mean(pre * pre, axis=-1, keepdims=True) + norm_eps) * gain
    flipped = jnp.concatenate([normed[:, half:], normed[:, :half]], axis=1)
    return normed * cosine + flipped * sine


def turn_back(pre, gain, cosine, sine, cotangent):
    scale = lax.rsqrt(jnp.mean(pre * pre, axis=-1, keepdims=True) + norm_eps)
    half = HD // 2
    flipped = jnp.concatenate([cotangent[:, half:], cotangent[:, :half]], axis=1)
    inner = (cotangent * cosine - flipped * sine) * gain
    return scale * inner - pre * (scale * scale * scale * jnp.mean(pre * inner, axis=-1, keepdims=True))


def attention(q_first, q_rest, mix, prompt, own_kv, cosine, sine, gain):
    rows, cols = mix.shape[0], mix.shape[1] - 2 * HD
    wide_cols = PAIR * HD
    count = KV_BLOCKS * rows
    specs, arrays = kv_specs(prompt, own_kv)
    flat = pl.BlockSpec((rows, wide_cols), lambda h: (0, h))

    def kernel(*refs):
        q_in, m_in, rest = refs[:4], refs[4], refs[5:]
        kv_in, rest = rest[:KV_BLOCKS], rest[KV_BLOCKS:]
        cos_ref, sin_ref, gain_ref = rest[:3]
        pre_ref, query_ref, mixed_ref, mixing_ref, acc_ref, sum_ref = rest[3:9]
        keys, values, flipped = rest[9:]

        @pl.when(pl.program_id(0) == 0)
        def _():
            acc_ref[...] = jnp.zeros_like(acc_ref)
            load_kv(kv_in, keys, values)
            flipped[...] = values[...].T
            total = sum(scalar_of(r[...].reshape(-1, 2 * HD)) for r in kv_in[:-1])
            sum_ref[...] = jnp.broadcast_to(total, sum_ref.shape)

        pre = sum(wide(r[...]) for r in q_in)
        mixing = m_in[...]
        stack = stack_heads(pre)
        pre_ref[...] = stack
        mixing_ref[...] = stack_heads(mixing)
        scale = lax.rsqrt(jnp.mean(stack * stack, axis=-1, keepdims=True) + norm_eps)
        cosine = jnp.concatenate([cos_ref[...]] * PAIR, axis=0)
        sine = jnp.concatenate([sin_ref[...]] * PAIR, axis=0)
        query = turn(stack * scale * gain_ref[...], cosine, sine).astype(BF)
        probs = probabilities(query, keys[...], rows)
        mixed = jnp.dot(flipped[...], probs.astype(BF), preferred_element_type=F32)
        mixed = lay_heads(mixed.T).astype(BF)
        query_ref[...] = query
        mixed_ref[...] = mixed
        terms = wide(mixed) * mixing
        acc_ref[...] += sum(terms[:, n * HD : (n + 1) * HD] for n in range(PAIR))

    heads = cols // HD
    wide_out = sds((heads * rows, HD), F32)
    low_out = sds((heads * rows, HD), BF)
    tall = pl.BlockSpec((PAIR * rows, HD), lambda h: (h, 0))
    return pl.pallas_call(
        kernel,
        grid=(cols // wide_cols,),
        in_specs=[flat] * 5
        + specs
        + [whole(v) for v in (cosine, sine, gain)],
        out_specs=[tall, tall, flat, tall]
        + [pl.BlockSpec((rows, HD), lambda h: (0, 0)), pl.BlockSpec((8, HD), lambda h: (0, 0))],
        out_shape=[wide_out, low_out, sds((rows, cols), BF), wide_out]
        + [sds((rows, HD), F32), sds((8, HD), F32)],
        scratch_shapes=[
            pltpu.VMEM((count, HD), BF),
            pltpu.VMEM((count, HD), BF),
            pltpu.VMEM((HD, count), BF),
        ],
        compiler_params=alone,
        cost_estimate=cost(8),
    )(q_first, *q_rest, mix, *arrays, cosine, sine, gain)


def attention_slopes(pre, query, mixing, prompt, own_kv, cosine, sine, gain):
    rows = own_kv.shape[0]
    cols = query.shape[0] // rows * HD
    wide_cols = PAIR * HD
    count = KV_BLOCKS * rows
    tall = pl.BlockSpec((PAIR * rows, HD), lambda h: (h, 0))
    across = pl.BlockSpec((count, PAIR * rows), lambda h: (0, h))
    specs, arrays = kv_specs(prompt, own_kv)

    def kernel(pre_ref, query_ref, mixing_ref, *refs):
        kv_in, rest = refs[:KV_BLOCKS], refs[KV_BLOCKS:]
        cos_ref, sin_ref, gain_ref, probs_ref, score_ref, back_ref, keys, values, flipped = rest

        @pl.when(pl.program_id(0) == 0)
        def _():
            load_kv(kv_in, keys, values)
            flipped[...] = keys[...].T

        query = query_ref[...]
        probs = probabilities(query, keys[...], rows)
        probs_ref[...] = probs.astype(BF)
        grad = mixing_ref[...].astype(BF)
        prob_cot = lax.dot_general(values[...], grad, NT, preferred_element_type=F32)
        inner = jnp.sum(probs * prob_cot, axis=0, keepdims=True)
        score_cot = (probs * (prob_cot - inner) * HD ** (-0.5)).astype(BF)
        score_ref[...] = score_cot
        query_cot = jnp.dot(flipped[...], score_cot, preferred_element_type=F32).T
        cosine = jnp.concatenate([cos_ref[...]] * PAIR, axis=0)
        sine = jnp.concatenate([sin_ref[...]] * PAIR, axis=0)
        back_ref[...] = lay_heads(
            turn_back(pre_ref[...], gain_ref[...], cosine, sine, query_cot)
        )

    return pl.pallas_call(
        kernel,
        grid=(cols // wide_cols,),
        in_specs=[tall] * 3 + specs + [whole(v) for v in (cosine, sine, gain)],
        out_specs=[across, across, pl.BlockSpec((rows, wide_cols), lambda h: (0, h))],
        out_shape=[sds((count, query.shape[0]), BF)] * 2 + [sds((rows, cols), F32)],
        scratch_shapes=[
            pltpu.VMEM((count, HD), BF),
            pltpu.VMEM((count, HD), BF),
            pltpu.VMEM((HD, count), BF),
        ],
        compiler_params=alone,
        cost_estimate=cost(8),
    )(pre, query, mixing, *arrays, cosine, sine, gain)


def attention_back(slope, probs, score_cot, back, query, mixing, cosine, sine, k_pre, k_gain):
    rows, cols = back.shape
    heads = cols // HD
    own_cols = cols + 2 * HD
    send_cols = own_cols + 4 * HD
    count = KV_BLOCKS * rows

    def kernel(slope_ref, probs_ref, score_ref, back_ref, query_ref, mixing_ref, *refs):
        cos_ref, sin_ref, k_pre_ref, k_gain_ref, own_ref, home_ref, *send_refs = refs
        slope = slope_ref[...]
        tall = jnp.concatenate([slope] * heads, axis=0)
        query = (tall * wide(query_ref[...])).astype(BF)
        grad = (tall * mixing_ref[...]).astype(BF)
        key_cot = jnp.dot(score_ref[...], query, preferred_element_type=F32)
        value_cot = jnp.dot(probs_ref[...], grad, preferred_element_type=F32)
        cots = jnp.concatenate([key_cot.astype(BF), value_cot.astype(BF)], axis=1)

        def block(n):
            return cots[n * rows : (n + 1) * rows]

        own_k = turn_back(
            k_pre_ref[...], k_gain_ref[...], cos_ref[...], sin_ref[...], key_cot[count - rows :]
        )
        own = jnp.concatenate(
            [(slope * back_ref[...]).astype(BF), own_k.astype(BF), block(2 * XS)[:, HD:]], axis=1
        )
        own_ref[...] = own
        for n in range(2):
            home_ref[n] = block(n)
        for dx in range(1, XS):
            send_ref = send_refs[dx - 1]
            send_ref[:, :own_cols] = own
            for n in range(2):
                at = own_cols + n * 2 * HD
                send_ref[:, at : at + 2 * HD] = block(2 * (XS - dx) + n)

    send_out = sds((rows, send_cols), BF)
    outs = [sds((rows, own_cols), BF), sds((2, rows, 2 * HD), BF)] + [send_out] * (XS - 1)
    inputs = (slope, probs, score_cot, back, query, mixing, cosine, sine, k_pre, k_gain)
    return pl.pallas_call(
        kernel,
        grid=(1,),
        in_specs=[whole(v) for v in inputs],
        out_specs=[whole(v) for v in outs],
        out_shape=outs,
        compiler_params=alone,
        cost_estimate=cost(4),
    )(*inputs)


def weight_grad(left, blocks, cols, tile):
    def kernel(left_ref, *refs):
        right = jnp.concatenate(
            [r[...].reshape(-1, tile) for r in refs[:-1]], axis=0
        )
        refs[-1][...] = jnp.dot(left_ref[...], right, preferred_element_type=F32).astype(BF)

    specs = [
        pl.BlockSpec(b.shape[:-1] + (tile,), lambda c, n=b.ndim: (0,) * (n - 1) + (c,)) for b in blocks
    ]
    return pl.pallas_call(
        kernel,
        grid=(cols // tile,),
        in_specs=[whole(left)] + specs,
        out_specs=pl.BlockSpec((left.shape[0], tile), lambda c: (0, c)),
        out_shape=sds((left.shape[0], cols), BF),
        compiler_params=params,
        cost_estimate=cost(3),
    )(left, *blocks)


def weight_grad_kv(order, left_x, blocks, left_p, prompt, kcols):
    tile = 2 * kcols
    rows, cols = blocks[0].shape
    at = cols // tile - 1
    count = len(blocks)

    def kernel(order_ref, x_ref, p_ref, *refs):
        k_ref, v_ref, sum_ref = refs[-3:]
        right = jnp.concatenate([r[...] for r in refs[:count]], axis=0)
        total = jnp.dot(x_ref[...], right, preferred_element_type=F32)
        more = [r[...].reshape(-1, tile) for r in refs[count:-3]]
        right = jnp.concatenate([m[:rows] for m in more], axis=0)
        total += jnp.dot(p_ref[...], right, preferred_element_type=F32)
        k_ref[...] = total[:, :kcols].astype(BF)
        v_ref[...] = total[:, kcols:].astype(BF)
        scalars = [scalar_of(m) for m in more]
        added = jnp.zeros((1, 1), F32)
        for device in range(count):
            added += sum(jnp.where(order_ref[n] == device, scalars[n], 0.0) for n in range(count))
        sum_ref[...] = jnp.broadcast_to(added, sum_ref.shape)

    specs = [pl.BlockSpec((rows, tile), lambda c, o: (0, at))] * count
    for array, index in prompt:
        if index is None:
            specs.append(pl.BlockSpec((rows + TAIL, tile), lambda c, o: (0, 0)))
        else:
            specs.append(
                pl.BlockSpec((1, rows + TAIL, tile), lambda c, o, index=index: (index, 0, 0))
            )
    narrow = sds((left_x.shape[0], kcols), BF)
    outs = [narrow, narrow, sds((8, HD), F32)]
    return pl.pallas_call(
        kernel,
        grid_spec=pltpu.PrefetchScalarGridSpec(
            num_scalar_prefetch=1,
            grid=(1,),
            in_specs=[whole(left_x), whole(left_p)] + specs,
            out_specs=[whole(v) for v in outs],
        ),
        out_shape=outs,
        compiler_params=params,
        cost_estimate=cost(3),
    )(order, left_x, left_p, *blocks, *[array for array, _ in prompt])


def tables(positions):
    half = HD // 2
    frequency = jnp.exp(jnp.arange(half, dtype=F32) * (-2.0 * math.log(rope_base) / HD))
    angles = positions[:, None] * frequency[None, :]
    cosine, sine = jnp.cos(angles), jnp.sin(angles)
    return jnp.concatenate([cosine, cosine], axis=1), jnp.concatenate([-sine, sine], axis=1)


def body(
    resp_hidden,
    prompt_hidden,
    readout,
    query_weight,
    key_weight,
    value_weight,
    out_weight,
    query_gain,
    key_gain,
    base_logprob,
    behavior_logprob,
    reference_logprob,
    rewards,
    lengths,
):
    own_x = resp_hidden[0]
    own_read = readout[0]
    rows = own_x.shape[0]
    qcols = query_weight.shape[1]
    kcols = key_weight.shape[1]
    groups = lax.axis_size("resp")
    index = lax.axis_index("resp").astype(jnp.int32)
    offset = jnp.arange(2 * XS, dtype=jnp.int32)
    order = ((index // 2 + offset % XS) % XS) * 2 + (index % 2 + offset // XS) % 2

    tokens = exchange(pack(prompt_hidden, own_read))
    tokens_x = exchange(pack(own_x))
    own_part = jnp.sum(wide(own_x) * wide(own_read), axis=-1)
    prompt_pos = (index * rows + jnp.arange(rows)).astype(F32)
    resp_pos = (rows * groups + jnp.arange(rows)).astype(F32)
    prompt_cos, prompt_sin = tables(prompt_pos)
    resp_cos, resp_sin = tables(resp_pos)

    kv_weight = jnp.concatenate([key_weight, value_weight], axis=1)
    qkv_weight = jnp.concatenate([query_weight, kv_weight], axis=1)
    at_x, at_y = index // 2, index % 2

    ready = (own_part, prompt_cos, prompt_sin, resp_cos, resp_sin, kv_weight, qkv_weight)
    ready, tokens = lax.optimization_barrier((ready, tokens))
    own_part, prompt_cos, prompt_sin, resp_cos, resp_sin, kv_weight, qkv_weight = ready

    m_parts = project(tokens[:, rows:], out_weight)
    kv_parts = project(tokens[:, :rows], kv_weight)
    pairs = []
    for n in range(XS):
        to = (at_x + n) % XS
        pairs.append(jnp.concatenate([pick(m_parts, to), pick(kv_parts, to)], axis=2))
    got_m = [send(pairs[n], n) for n in range(1, XS)]
    pairs, tokens, tokens_x = lax.optimization_barrier((pairs, tokens, tokens_x))
    q_parts = project(tokens_x, qkv_weight)
    far_q = pick(q_parts, 1 - at_y, 1)
    got_q = send(far_q, 0, 1)
    far_q, tokens, tokens_x = lax.optimization_barrier((far_q, tokens, tokens_x))
    flipped = flip_tokens(order, tokens_x, tokens)
    got_q, flipped = lax.optimization_barrier((got_q, flipped))
    left_x, left_p, left_r = flipped

    def half(n):
        to = (at_x + n) % XS
        return wide(pick(pick(q_parts, to), at_y)) + wide(pick(got_q, to))

    half_q = [half(n).astype(BF) for n in range(1, XS)]
    parts_q = [send(half_q[n - 1], n) for n in range(1, XS)]
    got_m, half_q = lax.optimization_barrier((got_m, half_q))
    every_m = [pairs[0]] + got_m
    far_m = sum(wide(pick(g, 1 - at_y)) for g in every_m).astype(BF)
    last_m = send(far_m, 0, 1)
    mix = sum(wide(pick(g, at_y)) for g in every_m) + wide(last_m)
    kv_pre = mix[:, qcols:]
    kp_pre = kv_pre[:, :kcols]
    prompt_keys = turn_rows(kp_pre, key_gain, prompt_cos, prompt_sin)
    kv_block = jnp.concatenate([prompt_keys.astype(BF), kv_pre[:, kcols:].astype(BF)], axis=1)
    kv_block = with_scalar(kv_block, rewards[0])
    other_kv = send(kv_block, 0, 1)
    parts_q, kv_block, other_kv = lax.optimization_barrier((parts_q, kv_block, other_kv))
    pair_kv = jnp.stack([kv_block, other_kv])
    got_kv = [send(pair_kv, n) for n in range(1, XS)]
    first_q = half(0)
    kvr_pre = first_q[:, qcols:] + sum(wide(part[:, qcols:]) for part in parts_q)
    kr_pre = kvr_pre[:, :kcols]
    resp_keys = turn_rows(kr_pre, key_gain, resp_cos, resp_sin)
    own_kv = jnp.concatenate([resp_keys.astype(BF), kvr_pre[:, kcols:].astype(BF)], axis=1)
    prompt_kv = [kv_block, other_kv] + got_kv

    q_gain, k_gain = query_gain[None, :], key_gain[None, :]
    q_pre, query, mixed, mixing, attn_acc, reward_sum = attention(
        first_q,
        parts_q,
        mix,
        prompt_kv,
        own_kv,
        resp_cos,
        resp_sin,
        q_gain,
    )
    probs, score_cot, back = attention_slopes(
        q_pre, query, mixing, prompt_kv, own_kv, resp_cos, resp_sin, q_gain
    )
    attn_logit = xor_sum(jnp.sum(attn_acc, axis=-1)[None, :], "head")[0]
    logprob = base_logprob[0] + own_part + attn_logit
    advantage = rewards[0] - reward_sum[0, 0] / groups
    live = (jnp.arange(rows) < lengths[0]).astype(F32)
    loss_own, lp_slope = objective(
        logprob, behavior_logprob[0], reference_logprob[0], advantage, live
    )
    mixing_grad = (lp_slope[:, None] * wide(mixed)).astype(BF)
    near_dm = [mixing_grad] + [send(mixing_grad, XS - n) for n in range(1, XS)]
    own_cots, home, *send_cots = attention_back(
        lp_slope[:, None],
        probs,
        score_cot,
        back,
        query,
        mixing,
        resp_cos,
        resp_sin,
        kr_pre,
        k_gain,
    )
    first_dm = send(mixing_grad, 0, 1)
    own_cots, home, send_cots, near_dm, first_dm = lax.optimization_barrier(
        (own_cots, home, send_cots, near_dm, first_dm)
    )
    got_d = [send(send_cots[n], n + 1) for n in range(XS - 1)]
    other_cots = send(own_cots, 0, 1)
    far_dm = send(jnp.stack(near_dm[1:]), 0, 1)
    got_d, other_cots, far_dm = lax.optimization_barrier((got_d, other_cots, far_dm))
    at = qcols + 2 * kcols
    far_kv = (wide(home[1]) + sum(wide(g[:, at + 2 * kcols :]) for g in got_d)).astype(BF)
    last_kv = send(far_kv, 0, 1)
    far_d = [send(other_cots, n) for n in range(1, XS)]
    dkv = wide(home[0]) + sum(wide(g[:, at : at + 2 * kcols]) for g in got_d) + wide(last_kv)
    dkp = turn_back(kp_pre, k_gain, prompt_cos, prompt_sin, dkv[:, :kcols])
    block_dp = jnp.concatenate([dkp.astype(BF), dkv[:, kcols:].astype(BF)], axis=1)
    block_dp = with_scalar(block_dp, loss_own)
    other_dp = send(block_dp, 0, 1)
    out_grad = weight_grad(left_r, near_dm + [first_dm, far_dm], qcols, 512)
    far_d, other_dp, out_grad = lax.optimization_barrier((far_d, other_dp, out_grad))
    pair_dp = jnp.stack([block_dp, other_dp])
    got_dp = [send(pair_dp, n) for n in range(1, XS)]
    by_offset = [2, 1, 0]
    cots = [own_cots] + [got_d[n] for n in by_offset]
    cots += [other_cots] + [far_d[n] for n in by_offset]
    query_grad = weight_grad(left_x, cots, qcols, 512)
    got_dp, query_grad = lax.optimization_barrier((got_dp, query_grad))
    prompt = [(block_dp, None)] + [(got_dp[n], 0) for n in by_offset]
    prompt += [(other_dp, None)] + [(got_dp[n], 1) for n in by_offset]
    key_grad, value_grad, loss = weight_grad_kv(order, left_x, cots, left_p, prompt, kcols)
    group_loss = loss[0, :1]
    return (
        logprob[None, :],
        group_loss,
        query_grad,
        key_grad,
        value_grad,
        out_grad,
    )


def solution(mesh):
    placed = (
        P(("grp", "resp"), None, None),
        P(("grp", "resp"), None),
        P(("grp", "resp"), None, None),
        P("resp", "head"),
        P("resp", "head"),
        P("resp", "head"),
        P("resp", "head"),
        P(),
        P(),
        P(("grp", "resp"), None),
        P(("grp", "resp"), None),
        P(("grp", "resp"), None),
        P(("grp", "resp")),
        P(("grp", "resp")),
    )
    return jax.shard_map(
        body,
        mesh=mesh,
        in_specs=placed,
        out_specs=(
            P(("grp", "resp"), None),
            P("grp"),
            P(("grp", "resp"), "head"),
            P(("grp", "resp"), "head"),
            P(("grp", "resp"), "head"),
            P(("grp", "resp"), "head"),
        ),
        check_vma=False,
    )
```
